512 devices in a mesh: leaf: 128 (over y, z, core), sub: 4 (over x).
Axes of the slice: x: 4, y: 4, z: 16, core: 2. Of those that a mesh axis runs over, the one named last changes fastest.
Arguments:
- leaf_bases: float32 [128, 4, 32, 64, 64], P('leaf', 'sub'), as said below
- local_transfer: float32 [128, 4, 62, 64, 64], P('leaf', 'sub')
- path_transfer: float32 [128, 4, 9, 64, 64], P('leaf', 'sub'), as said below
- leaf_points: float32 [128, 4, 32, 3, 64], P('leaf', 'sub'), may hold values from 0 to 1
- pair_rows: int32 [128, 4, 128], P('leaf', 'sub'), may hold values from 0 to 31
- pair_cols: int32 [128, 4, 128], P('leaf', 'sub'), may hold values from 0 to 63, as said below
- pair_offsets: int32 [128, 4, 3, 128], P('leaf', 'sub'), may hold values from -3 to 3, as said below
- send_slots: int32 [128, 4, 32], P('leaf', 'sub'), may hold values from 0 to 31, as said below
- send_counts: int32 [128, 4], P('leaf', 'sub'), may hold values from 1 to 32, as said below
Outputs:
- local_factors: float32 [128, 4, 63, 64, 64], P('leaf', 'sub')
- path_factors: float32 [128, 4, 9, 64, 64], P('leaf', 'sub')
- couplings: bfloat16 [128, 4, 128, 64, 64], P('leaf', 'sub')
The draws below stay inside these ranges and needn't reach their ends.
Inputs may be any that keep to these rules, and one draw needn't show every extreme that they name: path_transfer[L,s,j] is the same on all devices d = L * 4 + s with equal d >> j. `pair_offsets`: the first coordinate of every offset is 2, 3, -2 or -3. pair_cols names only neighbours that exist: below 32 never on leaf index 0, 32 or more never on leaf index 127. `send_slots`: the 32 entries of one device are distinct leaves. `send_counts`: 32 is reached in every draw. `leaf_bases`: bases and transfers are well conditioned, of full rank.
All inputs are finite; a program needn't handle non-finite values.
Results may differ from the reference program's by a relative error of at most 0.001.
Values sent between devices are 32-bit elements; how exact they have to be, the bound alone decides.
No kernel may reach another device: no remote copies, remote signals or barrier semaphores. Data moves between devices by JAX's collectives and lax.ppermute only.
A program may use at most 128 MiB of HBM per device.

```python
import math
import jax
import jax.numpy as jnp
from jax import lax

LEAF_SIZE = 64
RANK = 64
LEAF_DEV = 32
SEND = 32
CROSS = 9
PAIR_DEV = 128
NODES = 63
EDGES = 62
N_LEAF = 128
N_SUB = 4


def near_identity(noise, diagonal, sigma):
    rows = noise.shape[-2]
    cols = noise.shape[-1]
    return diagonal * jnp.eye(rows, cols, dtype=jnp.float32) + sigma * noise


def draw_leaf_bases(key, part):
    key = jax.random.fold_in(key, 11)
    shape = (N_LEAF, N_SUB, LEAF_DEV, LEAF_SIZE, RANK)
    sigma = 0.6 / math.sqrt(LEAF_SIZE)
    noise = jax.random.normal(key, shape, jnp.float32)
    return near_identity(noise, 2.0, sigma)


def draw_local_transfer(key, part):
    key = jax.random.fold_in(key, 12)
    shape = (N_LEAF, N_SUB, 2 * LEAF_DEV - 2, RANK, RANK)
    sigma = 0.24 / math.sqrt(RANK)
    noise = jax.random.normal(key, shape, jnp.float32)
    return near_identity(noise, math.sqrt(0.5 - 0.24 ** 2), sigma)


def draw_path_transfer(key, part):
    key = jax.random.fold_in(key, 13)
    dev_count = N_LEAF * N_SUB
    shape = (CROSS, dev_count, RANK, RANK)
    sigma = 0.24 / math.sqrt(RANK)
    table = jax.random.normal(key, shape, jnp.float32)
    devices = jnp.arange(dev_count, dtype=jnp.int32)
    levels = jnp.arange(CROSS, dtype=jnp.int32)
    owner = jnp.right_shift(devices[:, None], levels[None, :])
    picked = table[levels[None, :], owner]
    return near_identity(picked, math.sqrt(0.5 - 0.24 ** 2), sigma).reshape(N_LEAF, N_SUB, CROSS, RANK, RANK)


def draw_pair_cols(key, part):
    key = jax.random.fold_in(key, 17)
    side_key, slot_key = jax.random.split(key)
    side = jax.random.randint(side_key, (N_LEAF, N_SUB, PAIR_DEV), 0, 2)
    leaf_ids = jnp.arange(N_LEAF, dtype=jnp.int32)[:, None, None]
    side = jnp.where(leaf_ids == 0, 1, side)
    side = jnp.where(leaf_ids == N_LEAF - 1, 0, side)
    slot = jax.random.randint(slot_key, (N_LEAF, N_SUB, PAIR_DEV), 0, SEND)
    return (side * SEND + slot).astype(jnp.int32)


def draw_pair_offsets(key, part):
    key = jax.random.fold_in(key, 14)
    first_key, rest_key = jax.random.split(key)
    choice_val = jax.random.randint(first_key, (N_LEAF, N_SUB, 1, PAIR_DEV), 0, 4)
    first = (2 + choice_val % 2) * (1 - 2 * (choice_val // 2))
    rest = jax.random.randint(rest_key, (N_LEAF, N_SUB, 2, PAIR_DEV), -3, 4)
    return jnp.concatenate([first, rest], axis=2).astype(jnp.int32)


def draw_send_slots(key, part):
    key = jax.random.fold_in(key, 15)
    scores = jax.random.randint(key, (N_LEAF, N_SUB, LEAF_DEV), 0, 1 << 20) * LEAF_DEV
    scores = scores + jnp.arange(LEAF_DEV, dtype=jnp.int32)[None, None, :]
    order = jnp.argsort(scores, axis=-1)
    return order[:, :, :SEND].astype(jnp.int32)


def draw_send_counts(key, part):
    key = jax.random.fold_in(key, 16)
    base_key, pick_key = jax.random.split(key)
    base = jax.random.randint(base_key, (N_LEAF, N_SUB), max(1, SEND // 2), SEND + 1)
    chosen = jax.random.randint(pick_key, (), 0, N_LEAF)
    leaf_ids = jnp.arange(N_LEAF, dtype=jnp.int32)[:, None]
    return jnp.where(leaf_ids == chosen, SEND, base).astype(jnp.int32)


def with_ends(values, rng, smallest, largest):
    spot = [jax.random.randint(jax.random.fold_in(rng, axis), (), 0, length) for axis, length in enumerate(values.shape)]
    main_axis = values.shape.index(max(values.shape))
    next_to = spot[:main_axis] + [(spot[main_axis] + 1) % values.shape[main_axis]] + spot[main_axis + 1:]
    return values.at[tuple(spot)].set(smallest).at[tuple(next_to)].set(largest)


def level_of(own_key, extent, shards, least, top_value):
    loudness = 1.0
    for dim, shards_of in shards:
        draws = jax.random.uniform(jax.random.fold_in(jax.random.fold_in(own_key, 6), dim), (shards_of,), jnp.float32, least / len(shards), top_value / len(shards))
        loudness = loudness * jnp.repeat(jnp.exp(draws), extent[dim] // shards_of).reshape((-1,) + (1,) * (len(extent) - 1 - dim))
    return loudness


def setup_inputs(seed: int = 0) -> dict:
    splits = jax.random.split(jax.random.key(seed), 10)
    return {
        "leaf_bases": draw_leaf_bases(jax.random.fold_in(splits[9], 71), 0),
        "local_transfer": draw_local_transfer(jax.random.fold_in(splits[9], 71), 0),
        "path_transfer": draw_path_transfer(jax.random.fold_in(splits[9], 71), 0),
        "leaf_points": jnp.clip(1.0 * jax.random.uniform(splits[3], (N_LEAF, N_SUB, LEAF_DEV, 3, RANK), jnp.float32) ** level_of(splits[3], (N_LEAF, N_SUB, LEAF_DEV, 3, RANK), ((0, 128), (1, 4)), -0.2, 0.2), 0.0, 1.0),
        "pair_rows": with_ends(jax.random.randint(splits[4], (N_LEAF, N_SUB, PAIR_DEV), 0, LEAF_DEV), jax.random.fold_in(splits[4], 1), 0, LEAF_DEV - 1).astype(jnp.int32),
        "pair_cols": draw_pair_cols(jax.random.fold_in(splits[9], 71), 0),
        "pair_offsets": draw_pair_offsets(jax.random.fold_in(splits[9], 71), 0),
        "send_slots": draw_send_slots(jax.random.fold_in(splits[9], 71), 0),
        "send_counts": draw_send_counts(jax.random.fold_in(splits[9], 71), 0),
    }


exact_mode = lax.Precision.HIGHEST

def upper_factor(gram):
    return jnp.swapaxes(jnp.linalg.cholesky(gram), -1, -2)

def carry_up(gram, transfer):
    inner = jnp.einsum('...ik,...kl->...il', gram, transfer, precision=exact_mode)
    return jnp.einsum('...ki,...kl->...il', transfer, inner, precision=exact_mode)

def local_tree(bases, transfers):
    gram_now = jnp.einsum('nij,nik->njk', bases, bases, precision=exact_mode)
    grams = [gram_now]
    node_offset = 0
    node_count = bases.shape[0]
    while node_count > 1:
        carried = carry_up(gram_now, transfers[node_offset:node_offset + node_count])
        gram_now = carried[0::2] + carried[1::2]
        grams.append(gram_now)
        node_offset = node_offset + node_count
        node_count = node_count // 2
    return (upper_factor(jnp.concatenate(grams, 0)), gram_now[0])

def project_pairs(row_fac, row_pts, col_fac, col_pts, shift_vec):
    delta = row_pts[:, :, :, None] - col_pts[:, :, None, :] - shift_vec[:, :, None, None]
    kernel = 1.0 / jnp.sqrt(lax.optimization_barrier(jnp.sum(delta * delta, axis=1)))
    left = jnp.einsum('bij,bjk->bik', row_fac, kernel, precision=exact_mode)
    return jnp.einsum('bik,blk->bil', left, col_fac, precision=exact_mode).astype(jnp.bfloat16)

def reference(leaf_bases, local_transfer, path_transfer, leaf_points, pair_rows, pair_cols, pair_offsets, send_slots, send_counts):
    leaf_num, sub_num, leaf_count = (leaf_bases.shape[0], leaf_bases.shape[1], leaf_bases.shape[2])
    dev_count = leaf_num * sub_num
    bases = leaf_bases.reshape(dev_count, leaf_count, LEAF_SIZE, RANK)
    transfers = local_transfer.reshape(dev_count, EDGES, RANK, RANK)
    factors, roots = lax.map(lambda items: local_tree(items[0], items[1]), (bases, transfers))
    path_all = path_transfer.reshape(dev_count, CROSS, RANK, RANK)
    gram_now = roots
    level_out = []
    for level in range(1, CROSS + 1):
        stride_len = 2 ** (level - 1)
        carried = carry_up(gram_now, path_all[::stride_len, level - 1])
        gram_now = carried[0::2] + carried[1::2]
        level_out.append(jnp.repeat(upper_factor(gram_now), 2 ** level, axis=0))
    path_factors = jnp.stack(level_out, 1).reshape(leaf_num, sub_num, CROSS, RANK, RANK)
    flat_fac = factors[:, :leaf_count].reshape(dev_count * leaf_count, RANK, RANK)
    flat_pts = leaf_points.reshape(dev_count * leaf_count, 3, RANK)
    sub_ids = jnp.broadcast_to(jnp.arange(sub_num).astype(jnp.int32)[None, :, None], (leaf_num, sub_num, PAIR_DEV))
    leaf_ids = jnp.arange(leaf_num).astype(jnp.int32)[:, None, None]
    peer_ids = jnp.clip(leaf_ids - 1 + 2 * (pair_cols // SEND), 0, leaf_num - 1).astype(jnp.int32)
    slot_ids = (pair_cols % SEND).astype(jnp.int32)
    live_count = send_counts[peer_ids, sub_ids]
    pick_slot = jnp.minimum(slot_ids, live_count - 1).astype(jnp.int32)
    chosen = send_slots[peer_ids, sub_ids, pick_slot]
    col_index = ((peer_ids * sub_num + sub_ids) * leaf_count + chosen).reshape(dev_count, PAIR_DEV).astype(jnp.int32)
    dev_ids = jnp.arange(dev_count).astype(jnp.int32)[:, None]
    row_index = (dev_ids * leaf_count + pair_rows.reshape(dev_count, PAIR_DEV)).astype(jnp.int32)
    shift_all = jnp.swapaxes(pair_offsets.reshape(dev_count, 3, PAIR_DEV), 1, 2).astype(jnp.float32)

    def one_device(items):
        row_ids, col_ids, shift_vec = items
        return project_pairs(flat_fac[row_ids], flat_pts[row_ids], flat_fac[col_ids], flat_pts[col_ids], shift_vec)
    couplings = lax.map(one_device, (row_index, col_index, shift_all)).reshape(leaf_num, sub_num, PAIR_DEV, RANK, RANK)
    local_factors = factors.reshape(leaf_num, sub_num, NODES, RANK, RANK)
    return (local_factors, path_factors, couplings)
```

```python
import functools

import jax
import jax.numpy as jnp
from jax import lax
from jax.experimental import pallas as pl
from jax.experimental.pallas import tpu as pltpu
from jax.sharding import PartitionSpec as P

R = 64
W = 2 * R
f32 = jnp.float32
bf16 = jnp.bfloat16
VM = pl.BlockSpec(memory_space=pltpu.VMEM)
SM = pl.BlockSpec(memory_space=pltpu.SMEM)
LIMIT = 48 * 2**20


def dup(x):
    return jnp.concatenate([x, x], axis=1)


def lhs3(xd):
    lane = lax.broadcasted_iota(jnp.int32, xd.shape, 1)
    hi = xd.astype(bf16).astype(f32)
    both = jnp.where(lane < R, hi, xd - hi).astype(bf16)
    return jnp.concatenate([both, both[:, :R]], axis=1)


def rhs3(y):
    hi = y.astype(bf16)
    lo = (y - hi.astype(f32)).astype(bf16)
    return jnp.concatenate([hi, hi, lo], axis=0)


def mm(a, b):
    return jnp.dot(a, b, preferred_element_type=f32)


def carry(gd, e):
    inner = mm(lhs3(gd), rhs3(dup(e)))
    return mm(lhs3(dup(e.T)), rhs3(inner))


def pack(xd):
    lane = lax.broadcasted_iota(jnp.int32, (R // 2, W), 1)
    return jnp.where(lane < R, xd[: R // 2], xd[R // 2 :])


def unpack(x):
    lane = lax.broadcasted_iota(jnp.int32, (R // 2, W), 1)
    turned = jnp.concatenate([x[:, R:], x[:, :R]], axis=1)
    return jnp.concatenate([jnp.where(lane < R, x, turned), jnp.where(lane < R, turned, x)], axis=0)


def tree_kernel(nleaf, b_ref, e_ref, pe_ref, g_ref, c_ref, G):
    def leaf(n, _):
        b = b_ref[n]
        g = mm(lhs3(dup(b.T)), rhs3(dup(b)))
        G[n] = g
        g_ref[n] = g[:, :R]
        return _

    lax.fori_loop(0, nleaf, leaf, 0, unroll=4)
    off, cnt = 0, nleaf
    while cnt > 1:
        nxt = off + cnt

        def node(i, _, off=off, nxt=nxt):
            left = off + 2 * i
            s = carry(G[left], e_ref[left]) + carry(G[left + 1], e_ref[left + 1])
            G[nxt + i] = s
            g_ref[nxt + i] = s[:, :R]
            return _

        lax.fori_loop(0, cnt // 2, node, 0, unroll=min(4, cnt // 2))
        off, cnt = nxt, cnt // 2
    c_ref[...] = pack(carry(G[off], pe_ref[0]))


def tree(bases, transfers, path):
    n = bases.shape[0]
    return pl.pallas_call(
        functools.partial(tree_kernel, n),
        out_shape=(
            jax.ShapeDtypeStruct((2 * n - 1, R, R), f32),
            jax.ShapeDtypeStruct((R // 2, W), f32),
        ),
        in_specs=[VM, VM, VM],
        out_specs=(VM, VM),
        scratch_shapes=[pltpu.VMEM((2 * n - 1, R, W), f32)],
        compiler_params=pltpu.CompilerParams(vmem_limit_bytes=LIMIT),
        cost_estimate=pl.CostEstimate(flops=10**8, bytes_accessed=10**7, transcendentals=0),
        name="tree",
    )(bases, transfers, path)


def chol_core(T, lanes, blk=4):
    for b in range(R // blk):
        k0 = b * blk
        j0 = (k0 // 8) * 8
        n = R - j0
        acc = [T[pl.ds((k0 + r) * R + j0, n), :] for r in range(blk)]
        if k0 > 0:

            def step(i, acc, k0=k0, j0=j0, n=n):
                base = pl.multiple_of(i * R, R)
                row = T[pl.ds(base + j0, n), :]
                return tuple(acc[r] - T[pl.ds(base + k0 + r, 1), :] * row for r in range(blk))

            acc = list(lax.fori_loop(0, k0, step, tuple(acc), unroll=4))
        col = lax.broadcasted_iota(jnp.int32, (n, lanes), 0) + j0
        for r in range(blk):
            k = k0 + r
            row = acc[r] * lax.rsqrt(acc[r][k - j0 : k - j0 + 1, :])
            row = jnp.where(col >= k, row, 0.0)
            T[pl.ds(k * R + j0, n), :] = row
            if j0 > 0:
                T[pl.ds(k * R, j0), :] = jnp.zeros((j0, lanes), f32)
            for r2 in range(r + 1, blk):
                s = row[k0 + r2 - j0 : k0 + r2 - j0 + 1, :]
                acc[r2] = acc[r2] - s * row


def local_chol_kernel(nleaf, nb, slots, count, g_ref, p_ref, o_ref, k_ref, T, S, PT):
    S[pl.ds(0, nb * R), :] = g_ref[...]
    S[pl.ds(nb * R, R), :] = g_ref[pl.ds(0, R), :]
    lanes = nb + 1
    for i in range(R):
        T[pl.ds(i * R, R), :] = S[pl.ds(i, lanes, stride=R), :].T
    chol_core(T, lanes)
    for i in range(R):
        o_ref[pl.ds(i, nb, stride=R), :] = T[pl.ds(i * R, R), :].T[:nb]
    half = nleaf // 2

    def put(n, _):
        at = pl.multiple_of(n * R, R)
        k_ref[pl.ds(at, R), :] = jnp.concatenate(
            [o_ref[pl.ds(at, R), :], o_ref[pl.ds(at + half * R, R), :]], axis=1
        )
        return _

    lax.fori_loop(0, half, put, 0, unroll=4)
    for r in range(nleaf):
        PT[3 * r : 3 * r + 3, :] = p_ref[r]
    points = 3 * half
    k_ref[half * R : half * R + points, :] = jnp.concatenate([PT[:points], PT[points:]], axis=1)
    lane = lax.broadcasted_iota(jnp.int32, (8, W), 1)
    chosen = jnp.zeros((8, W), f32)
    live = count[0, 0]
    nslot = slots.shape[1]
    for s in range(nslot):
        leaf = slots[0, jnp.minimum(s, live - 1)]
        chosen = jnp.where(lane == s, leaf.astype(f32), chosen)
    k_ref[half * R + points : half * R + points + 8, :] = chosen


def local_chol(slots, count, grams, points):
    nb = grams.shape[0]
    nleaf = points.shape[0]
    rows = nleaf // 2 * R + 3 * nleaf // 2 + 8
    out, packet = pl.pallas_call(
        functools.partial(local_chol_kernel, nleaf, nb),
        out_shape=(
            jax.ShapeDtypeStruct((nb * R, R), f32),
            jax.ShapeDtypeStruct((rows, W), f32),
        ),
        in_specs=[SM, SM, VM, VM],
        out_specs=(VM, VM),
        scratch_shapes=[
            pltpu.VMEM((R * R, nb + 1), f32),
            pltpu.VMEM(((nb + 1) * R, R), f32),
            pltpu.VMEM((3 * nleaf, R), f32),
        ],
        compiler_params=pltpu.CompilerParams(vmem_limit_bytes=LIMIT),
        cost_estimate=pl.CostEstimate(flops=10**8, bytes_accessed=10**7, transcendentals=0),
        name="local_chol",
    )(slots, count, grams.reshape(nb * R, R), points)
    return out.reshape(nb, R, R), packet


def level_kernel(a_ref, b_ref, e_ref, h_ref, c_ref):
    h = unpack(a_ref[...] + b_ref[...])
    h_ref[...] = h
    c_ref[...] = pack(carry(h, e_ref[0]))


def level_step(own, other, path, level):
    return pl.pallas_call(
        level_kernel,
        grid=(1,),
        out_shape=(jax.ShapeDtypeStruct((R, W), f32), jax.ShapeDtypeStruct((R // 2, W), f32)),
        in_specs=[
            pl.BlockSpec((R // 2, W), lambda i: (0, 0)),
            pl.BlockSpec((R // 2, W), lambda i: (0, 0)),
            pl.BlockSpec((1, R, R), lambda i: (level, 0, 0)),
        ],
        out_specs=(
            pl.BlockSpec((R, W), lambda i: (0, 0)),
            pl.BlockSpec((R // 2, W), lambda i: (0, 0)),
        ),
        cost_estimate=pl.CostEstimate(flops=10**6, bytes_accessed=10**6, transcendentals=0),
        name="level_step",
    )(own, other, path)


def path_chol_kernel(levels, lanes, *refs):
    o_ref, T, S = refs[-3:]
    for n in range(levels - 1):
        S[pl.ds(n * R, R), :] = refs[n][:, :R]
    last = unpack(refs[levels - 1][...] + refs[levels][...])[:, :R]
    for n in range(levels - 1, lanes):
        S[pl.ds(n * R, R), :] = last
    for i in range(R):
        T[pl.ds(i * R, R), :] = S[pl.ds(i, lanes, stride=R), :].T
    chol_core(T, lanes)
    for i in range(R):
        o_ref[pl.ds(i, levels, stride=R), :] = T[pl.ds(i * R, R), :].T[:levels]


def path_chol(grams, own, other):
    levels = len(grams) + 1
    lanes = (levels + 7) // 8 * 8
    out = pl.pallas_call(
        functools.partial(path_chol_kernel, levels, lanes),
        out_shape=jax.ShapeDtypeStruct((levels * R, R), f32),
        in_specs=[VM] * (levels + 1),
        out_specs=VM,
        scratch_shapes=[pltpu.VMEM((R * R, lanes), f32), pltpu.VMEM((lanes * R, R), f32)],
        compiler_params=pltpu.CompilerParams(vmem_limit_bytes=LIMIT),
        cost_estimate=pl.CostEstimate(flops=10**7, bytes_accessed=10**6, transcendentals=0),
        name="path_chol",
    )(*grams, own, other)
    return out.reshape(levels, R, R)


def pairs_kernel(
    nleaf, npair, odd, rows, cols, offs, f_ref, a_ref, b_ref, o_ref, RL, CR, PB, QD, table, spot, sem
):
    half = nleaf // 2
    points = 3 * half
    nslot = nleaf
    for side, k_ref in enumerate((a_ref, b_ref)):
        spot[side] = k_ref[half * R + points : half * R + points + 8, :].astype(jnp.int32)
    copy = pltpu.make_async_copy(spot, table, sem)
    copy.start()

    def prep_row(r, _):
        RL[r] = lhs3(dup(f_ref[r]))
        return _

    lax.fori_loop(0, nleaf, prep_row, 0, unroll=4)
    for side, k_ref in enumerate((a_ref, b_ref)):

        def prep_col(n, _, side=side, k_ref=k_ref):
            both = k_ref[pl.ds(pl.multiple_of(n * R, R), R), :].T
            CR[side * nleaf + n] = rhs3(both[:R])
            CR[side * nleaf + half + n] = rhs3(both[R:])
            return _

        lax.fori_loop(0, half, prep_col, 0, unroll=4)
        q = k_ref[half * R : half * R + points, :]
        turned = jnp.concatenate([q[:, R:], q[:, :R]], axis=1)
        lane = lax.broadcasted_iota(jnp.int32, q.shape, 1)
        QD[side * 2 * points : side * 2 * points + points, :] = jnp.where(lane < R, q, turned)
        QD[side * 2 * points + points : (side + 1) * 2 * points, :] = jnp.where(lane < R, turned, q)
    copy.wait()

    def pair(k, _):
        r = rows[0, k]
        v = cols[0, k]
        right = v // nslot
        side = jnp.where(odd[0] == 1, right, 1 - right)
        c = side * nleaf + table[side, 0, v % nslot]
        d2 = None
        for a in range(3):
            q = QD[pl.ds(3 * c + a, 1), :] + offs[a, k].astype(f32)
            d = PB[3 * r + a] - q
            d2 = d * d if d2 is None else d2 + d * d
        left = mm(lhs3(lax.rsqrt(d2)), CR[c])
        o_ref[k] = mm(RL[r], rhs3(left)).astype(bf16)
        return _

    lax.fori_loop(0, npair, pair, 0, unroll=4)


def row_points(nleaf, p_ref, PB):
    for r in range(nleaf):
        pt = p_ref[r].T
        for a in range(3):
            PB[3 * r + a] = jnp.broadcast_to(pt[:, a : a + 1], (R, W))


def pairs_full(nleaf, npair, odd, rows, cols, offs, f_ref, p_ref, a_ref, b_ref, o_ref, RL, CR, PB, QD, table, spot, sem):
    row_points(nleaf, p_ref, PB)
    pairs_kernel(nleaf, npair, odd, rows, cols, offs, f_ref, a_ref, b_ref, o_ref, RL, CR, PB, QD, table, spot, sem)


def pairs(odd, rows, cols, offs, factors, points, first, second):
    npair = rows.shape[1]
    nleaf = points.shape[0]
    whole = lambda s: pl.BlockSpec(s, lambda i: (0,) * len(s))
    return pl.pallas_call(
        functools.partial(pairs_full, nleaf, npair),
        grid=(1,),
        out_shape=jax.ShapeDtypeStruct((npair, R, R), bf16),
        in_specs=[SM, SM, SM, SM]
        + [whole((nleaf, R, R)), whole(points.shape), whole(first.shape), whole(second.shape)],
        out_specs=whole((npair, R, R)),
        scratch_shapes=[
            pltpu.VMEM((nleaf, R, 3 * R), bf16),
            pltpu.VMEM((2 * nleaf, 3 * R, R), bf16),
            pltpu.VMEM((3 * nleaf, R, W), f32),
            pltpu.VMEM((6 * nleaf, W), f32),
            pltpu.SMEM((2, 8, W), jnp.int32),
            pltpu.VMEM((2, 8, W), jnp.int32),
            pltpu.SemaphoreType.DMA,
        ],
        compiler_params=pltpu.CompilerParams(vmem_limit_bytes=LIMIT),
        cost_estimate=pl.CostEstimate(flops=10**8, bytes_accessed=10**7, transcendentals=0),
        name="pairs",
    )(odd, rows, cols, offs, factors, points, first, second)


def partner(block, axis, bit):
    count = lax.axis_size(axis)
    return lax.ppermute(block, axis, [(i, i ^ (1 << bit)) for i in range(count)])


def body(
    leaf_bases,
    local_transfer,
    path_transfer,
    leaf_points,
    pair_rows,
    pair_cols,
    pair_offsets,
    send_slots,
    send_counts,
):
    path = path_transfer[0, 0]
    points = leaf_points[0, 0]
    grams, own = tree(leaf_bases[0, 0], local_transfer[0, 0], path)
    factors, packet = local_chol(send_slots[0], send_counts, grams, points)

    count = lax.axis_size("leaf")
    inside = [(i, i ^ 1) for i in range(count)]
    across = []
    for i in range(1, count - 1, 2):
        across += [(i, i + 1), (i + 1, i)]
    first = lax.ppermute(packet, "leaf", inside)
    second = lax.ppermute(packet, "leaf", across)

    steps = [("sub", b) for b in range(lax.axis_size("sub").bit_length() - 1)]
    steps += [("leaf", b) for b in range(count.bit_length() - 1)]
    level_grams = []
    for level, (axis, bit) in enumerate(steps):
        other = partner(own, axis, bit)
        if level + 1 < len(steps):
            gram, own = level_step(own, other, path, level + 1)
            level_grams.append(gram)
    path_factors = path_chol(level_grams, own, other)

    odd = (lax.axis_index("leaf") % 2).astype(jnp.int32).reshape(1)
    couplings = pairs(
        odd, pair_rows[0], pair_cols[0], pair_offsets[0, 0], factors, points, first, second
    )
    return (factors[None, None], path_factors[None, None], couplings[None, None])


def solution(mesh):
    wide = P("leaf", "sub", None, None, None)
    in_specs = (
        wide,
        wide,
        wide,
        wide,
        P("leaf", "sub", None),
        P("leaf", "sub", None),
        P("leaf", "sub", None, None),
        P("leaf", "sub", None),
        P("leaf", "sub"),
    )
    return jax.shard_map(body, mesh=mesh, in_specs=in_specs, out_specs=(wide, wide, wide), check_vma=False)
```

```python
import functools

import jax
import jax.numpy as jnp
from jax import lax
from jax.experimental import pallas as pl
from jax.experimental.pallas import tpu as pltpu
from jax.sharding import Mesh
from jax.sharding import PartitionSpec as P

R = 64
W = 2 * R
f32 = jnp.float32
bf16 = jnp.bfloat16
VM = pl.BlockSpec(memory_space=pltpu.VMEM)
HB = pl.BlockSpec(memory_space=pltpu.HBM)
SM = pl.BlockSpec(memory_space=pltpu.SMEM)
LIMIT = 48 * 2**20


def dup(x):
    return jnp.concatenate([x, x], axis=1)


def lhs3(xd):
    lane = lax.broadcasted_iota(jnp.int32, xd.shape, 1)
    hi = xd.astype(bf16).astype(f32)
    both = jnp.where(lane < R, hi, xd - hi).astype(bf16)
    return jnp.concatenate([both, both[:, :R]], axis=1)


def rhs3(y):
    hi = y.astype(bf16)
    lo = (y - hi.astype(f32)).astype(bf16)
    return jnp.concatenate([hi, hi, lo], axis=0)


def mm(a, b):
    return jnp.dot(a, b, preferred_element_type=f32)


def carry(gd, e):
    inner = mm(lhs3(gd), rhs3(dup(e)))
    return mm(lhs3(dup(e.T)), rhs3(inner))


def pack(xd):
    lane = lax.broadcasted_iota(jnp.int32, (R // 2, W), 1)
    return jnp.where(lane < R, xd[: R // 2], xd[R // 2 :])


def unpack(x):
    lane = lax.broadcasted_iota(jnp.int32, (R // 2, W), 1)
    turned = jnp.concatenate([x[:, R:], x[:, :R]], axis=1)
    return jnp.concatenate([jnp.where(lane < R, x, turned), jnp.where(lane < R, turned, x)], axis=0)


def send(levels, me, h, transfers, K, s_ref):
    for i in range(levels):
        h = carry(h, transfers[i])
        K[i] = pack(h)
    for p in range(2**levels):
        apart = me ^ p
        meet = jnp.int32(0)
        for i in range(1, levels):
            meet = meet + (apart >= 2**i).astype(jnp.int32)
        s_ref[p] = K[meet]
    return K[0]


def receive(levels, me, own, r_ref, transfers):
    grams = []
    for i in range(levels):
        first = ((me >> i) ^ 1) << i
        s = r_ref[first]
        for t in range(1, 2**i):
            s = s + r_ref[first + t]
        if i == 0:
            grams.append(unpack(s + own))
        else:
            grams.append(carry(grams[-1], transfers[i]) + unpack(s))
    return grams


def tree_kernel(nleaf, axes, levels, b_hbm, e_hbm, p_hbm, g_ref, s_ref, own_ref, G, B, E, F, K, sem):
    copies = [
        pltpu.make_async_copy(b_hbm, B, sem.at[0]),
        pltpu.make_async_copy(e_hbm.at[pl.ds(0, nleaf)], E.at[pl.ds(0, nleaf)], sem.at[1]),
        pltpu.make_async_copy(e_hbm.at[pl.ds(nleaf, nleaf - 2)], E.at[pl.ds(nleaf, nleaf - 2)], sem.at[2]),
        pltpu.make_async_copy(p_hbm.at[pl.ds(0, levels)], F, sem.at[3]),
    ]
    for copy in copies:
        copy.start()
    copies[0].wait()
    wide = 8

    def leaf(t, _):
        held = [B[t * wide + u] for u in range(wide)]
        out = [mm(lhs3(dup(b.T)), rhs3(dup(b))) for b in held]
        for u in range(wide):
            G[t * wide + u] = out[u]
            g_ref[t * wide + u] = out[u][:, :R]
        return _

    lax.fori_loop(0, nleaf // wide, leaf, 0)
    copies[1].wait()
    off, cnt = 0, nleaf
    while cnt > 1:
        if off == nleaf:
            copies[2].wait()
        nxt = off + cnt
        part = min(4, cnt // 2)

        def node(t, _, off=off, nxt=nxt, part=part):
            below = off + 2 * part * t
            held = [(G[below + u], E[below + u]) for u in range(2 * part)]
            out = [carry(g, e) for g, e in held]
            for u in range(part):
                s = out[2 * u] + out[2 * u + 1]
                G[nxt + part * t + u] = s
                g_ref[nxt + part * t + u] = s[:, :R]
            return _

        if cnt // 2 > part:
            lax.fori_loop(0, cnt // 2 // part, node, 0)
        else:
            node(0, 0)
        off, cnt = nxt, cnt // 2
    g_ref[off + 1] = G[off][:, :R]
    copies[3].wait()
    own_ref[...] = send(levels, lax.axis_index(axes), G[off], [F[i] for i in range(levels)], K, s_ref)


def tree(bases, transfers, path, axes, levels):
    n = bases.shape[0]
    return pl.pallas_call(
        functools.partial(tree_kernel, n, axes, levels),
        out_shape=(
            jax.ShapeDtypeStruct((2 * n, R, R), f32),
            jax.ShapeDtypeStruct((2**levels, R // 2, W), f32),
            jax.ShapeDtypeStruct((R // 2, W), f32),
        ),
        in_specs=[HB, HB, HB],
        out_specs=(VM, VM, VM),
        scratch_shapes=[
            pltpu.VMEM((2 * n - 1, R, W), f32),
            pltpu.VMEM((n, R, R), f32),
            pltpu.VMEM((2 * n - 2, R, R), f32),
            pltpu.VMEM((levels, R, R), f32),
            pltpu.VMEM((levels, R // 2, W), f32),
            pltpu.SemaphoreType.DMA((4,)),
        ],
        compiler_params=pltpu.CompilerParams(vmem_limit_bytes=LIMIT),
        cost_estimate=pl.CostEstimate(flops=10**8, bytes_accessed=10**7, transcendentals=0),
        name="tree",
    )(bases, transfers, path)


def chol_core(T, lanes, blk=4):
    for b in range(R // blk):
        k0 = b * blk
        j0 = (k0 // 8) * 8
        n = R - j0
        acc = [T[pl.ds((k0 + r) * R + j0, n), :] for r in range(blk)]
        if k0 > 0:

            def step(i, acc, k0=k0, j0=j0, n=n):
                base = pl.multiple_of(i * R, R)
                row = T[pl.ds(base + j0, n), :]
                return tuple(acc[r] - T[pl.ds(base + k0 + r, 1), :] * row for r in range(blk))

            acc = list(lax.fori_loop(0, k0, step, tuple(acc), unroll=4))
        col = lax.broadcasted_iota(jnp.int32, (n, lanes), 0) + j0
        for r in range(blk):
            k = k0 + r
            row = acc[r] * lax.rsqrt(acc[r][k - j0 : k - j0 + 1, :])
            row = jnp.where(col >= k, row, 0.0)
            T[pl.ds(k * R + j0, n), :] = row
            if j0 > 0:
                T[pl.ds(k * R, j0), :] = jnp.zeros((j0, lanes), f32)
            for r2 in range(r + 1, blk):
                s = row[k0 + r2 - j0 : k0 + r2 - j0 + 1, :]
                acc[r2] = acc[r2] - s * row


def local_chol_kernel(nleaf, nb, slots, count, g_ref, p_ref, o_ref, k_ref, T, PT):
    lanes = nb + 1
    for i in range(R):
        T[pl.ds(i * R, R), :] = g_ref[pl.ds(i, lanes, stride=R), :].T
    chol_core(T, lanes)
    for i in range(R):
        o_ref[pl.ds(i, nb, stride=R), :] = T[pl.ds(i * R, R), :].T[:nb]
    half = nleaf // 2

    def put(n, _):
        at = pl.multiple_of(n * R, R)
        k_ref[pl.ds(at, R), :] = jnp.concatenate(
            [o_ref[pl.ds(at, R), :], o_ref[pl.ds(at + half * R, R), :]], axis=1
        )
        return _

    lax.fori_loop(0, half, put, 0, unroll=4)
    for r in range(nleaf):
        PT[3 * r : 3 * r + 3, :] = p_ref[r]
    points = 3 * half
    k_ref[half * R : half * R + points, :] = jnp.concatenate([PT[:points], PT[points:]], axis=1)
    lane = lax.broadcasted_iota(jnp.int32, (8, W), 1)
    chosen = jnp.zeros((8, W), f32)
    live = count[0, 0]
    nslot = slots.shape[1]
    for s in range(nslot):
        leaf = slots[0, jnp.minimum(s, live - 1)]
        chosen = jnp.where(lane == s, leaf.astype(f32), chosen)
    k_ref[half * R + points : half * R + points + 8, :] = chosen


def local_chol(slots, count, grams, points):
    nb = grams.shape[0] - 1
    nleaf = points.shape[0]
    rows = nleaf // 2 * R + 3 * nleaf // 2 + 8
    out, packet = pl.pallas_call(
        functools.partial(local_chol_kernel, nleaf, nb),
        out_shape=(
            jax.ShapeDtypeStruct((nb * R, R), f32),
            jax.ShapeDtypeStruct((rows, W), f32),
        ),
        in_specs=[SM, SM, VM, VM],
        out_specs=(VM, VM),
        scratch_shapes=[pltpu.VMEM((R * R, nb + 1), f32), pltpu.VMEM((3 * nleaf, R), f32)],
        compiler_params=pltpu.CompilerParams(vmem_limit_bytes=LIMIT),
        cost_estimate=pl.CostEstimate(flops=10**8, bytes_accessed=10**7, transcendentals=0),
        name="local_chol",
    )(slots, count, grams.reshape((nb + 1) * R, R), points)
    return out.reshape(nb, R, R), packet


def group_kernel(axes, levels, base, axes2, levels2, r_ref, own_ref, e_ref, h_ref, s_ref, next_ref, K):
    fs = [e_ref[base + i] for i in range(levels + levels2)]
    grams = receive(levels, lax.axis_index(axes), own_ref[...], r_ref, fs[:levels])
    for i in range(levels):
        h_ref[i] = grams[i][:, :R]
    next_ref[...] = send(levels2, lax.axis_index(axes2), grams[-1], fs[levels:], K, s_ref)


def group_step(axes, levels, base, axes2, levels2, received, own, path):
    return pl.pallas_call(
        functools.partial(group_kernel, axes, levels, base, axes2, levels2),
        out_shape=(
            jax.ShapeDtypeStruct((levels, R, R), f32),
            jax.ShapeDtypeStruct((2**levels2, R // 2, W), f32),
            jax.ShapeDtypeStruct((R // 2, W), f32),
        ),
        in_specs=[VM, VM, VM],
        out_specs=(VM, VM, VM),
        scratch_shapes=[pltpu.VMEM((levels2, R // 2, W), f32)],
        cost_estimate=pl.CostEstimate(flops=10**7, bytes_accessed=10**6, transcendentals=0),
        name="group_step",
    )(received, own, path)


def path_chol_kernel(axes, levels, base, counts, *refs):
    r_ref, own_ref, e_ref = refs[:3]
    o_ref, T, S = refs[-3:]
    done = 0
    for count, ref in zip(counts, refs[3:-3]):
        for n in range(count):
            S[pl.ds((done + n) * R, R), :] = ref[n]
        done += count
    fs = [e_ref[base + i] for i in range(levels)]
    grams = receive(levels, lax.axis_index(axes), own_ref[...], r_ref, fs)
    total = done + levels
    lanes = S.shape[0] // R
    for n in range(done, lanes):
        S[pl.ds(n * R, R), :] = grams[min(n - done, levels - 1)][:, :R]
    for i in range(R):
        T[pl.ds(i * R, R), :] = S[pl.ds(i, lanes, stride=R), :].T
    chol_core(T, lanes)
    for i in range(R):
        o_ref[pl.ds(i, total, stride=R), :] = T[pl.ds(i * R, R), :].T[:total]


def path_chol(axes, levels, base, received, own, path, grams):
    counts = [g.shape[0] for g in grams]
    total = sum(counts) + levels
    lanes = (total + 7) // 8 * 8
    out = pl.pallas_call(
        functools.partial(path_chol_kernel, axes, levels, base, counts),
        out_shape=jax.ShapeDtypeStruct((total * R, R), f32),
        in_specs=[VM] * (3 + len(grams)),
        out_specs=VM,
        scratch_shapes=[pltpu.VMEM((R * R, lanes), f32), pltpu.VMEM((lanes * R, R), f32)],
        compiler_params=pltpu.CompilerParams(vmem_limit_bytes=LIMIT),
        cost_estimate=pl.CostEstimate(flops=10**7, bytes_accessed=10**6, transcendentals=0),
        name="path_chol",
    )(received, own, path, *grams)
    return out.reshape(total, R, R)


def halves(x):
    lane = lax.broadcasted_iota(jnp.int32, x.shape, 1)
    turned = jnp.concatenate([x[:, R:], x[:, :R]], axis=1)
    return jnp.where(lane < R, x, turned), jnp.where(lane < R, turned, x)


def pairs_kernel(
    nleaf, npair, rows, cols, offs, k_ref, a_ref, b_ref, o_hbm, RL, CR, PB, QD, S, OT, table, spot, sem, out_sem
):
    half = nleaf // 2
    points = 3 * half
    mark = half * R + points
    for side, r_ref in enumerate((a_ref, b_ref)):
        spot[side] = r_ref[mark : mark + 8, :].astype(jnp.int32)
    copy = pltpu.make_async_copy(spot, table, sem)
    copy.start()

    def prep_row(n, _):
        one, two = halves(k_ref[pl.ds(pl.multiple_of(n * R, R), R), :])
        RL[n] = lhs3(one)
        RL[half + n] = lhs3(two)
        return _

    lax.fori_loop(0, half, prep_row, 0, unroll=4)
    pt = k_ref[half * R : mark, :].T
    for r in range(points):
        PB[r] = jnp.broadcast_to(pt[:R, r : r + 1], (R, W))
        PB[points + r] = jnp.broadcast_to(pt[R:, r : r + 1], (R, W))
    for side, r_ref in enumerate((a_ref, b_ref)):

        def prep_col(n, _, side=side, r_ref=r_ref):
            both = r_ref[pl.ds(pl.multiple_of(n * R, R), R), :].T
            CR[side * nleaf + n] = rhs3(both[:R])
            CR[side * nleaf + half + n] = rhs3(both[R:])
            return _

        lax.fori_loop(0, half, prep_col, 0, unroll=4)
        one, two = halves(r_ref[half * R : mark, :])
        QD[side * 2 * points : side * 2 * points + points, :] = one
        QD[side * 2 * points + points : (side + 1) * 2 * points, :] = two
    copy.wait()
    odd = lax.axis_index("core")
    wide = 8

    def block(t, _):
        ks = [t * wide + u for u in range(wide)]
        rs = [rows[0, k] for k in ks]
        cs = []
        for k in ks:
            v = cols[0, k]
            right = v // nleaf
            side = jnp.where(odd == 1, right, 1 - right)
            cs.append(side * nleaf + table[side, 0, v % nleaf])
        kd = []
        for k, r, c in zip(ks, rs, cs):
            d2 = None
            for a in range(3):
                q = QD[pl.ds(3 * c + a, 1), :] + offs[a, k].astype(f32)
                d = PB[3 * r + a] - q
                d2 = d * d if d2 is None else d2 + d * d
            kd.append(lax.rsqrt(d2))
        left = [mm(lhs3(x), CR[c]) for x, c in zip(kd, cs)]
        out = [mm(RL[r], rhs3(x)) for x, r in zip(left, rs)]
        for u in range(wide):
            S[pl.ds(pl.multiple_of(ks[u] * R, R), R), :] = out[u]
        return _

    lax.fori_loop(0, npair // wide, block, 0)
    parts = 4
    rows_each = R // parts
    copies = []
    for c in range(parts):
        for i in range(c * rows_each, (c + 1) * rows_each):
            OT[i] = S[pl.ds(i, npair, stride=R), :].T.astype(bf16)
        at = pl.ds(c * rows_each, rows_each)
        copies.append(pltpu.make_async_copy(OT.at[at], o_hbm.at[at], out_sem.at[c]))
        copies[-1].start()
    for copy in copies:
        copy.wait()


def pairs(rows, cols, offs, packet, first, second, nleaf):
    npair = rows.shape[1]
    out = pl.pallas_call(
        functools.partial(pairs_kernel, nleaf, npair),
        out_shape=jax.ShapeDtypeStruct((R, R, npair), bf16),
        in_specs=[SM, SM, SM, VM, VM, VM],
        out_specs=HB,
        scratch_shapes=[
            pltpu.VMEM((nleaf, R, 3 * R), bf16),
            pltpu.VMEM((2 * nleaf, 3 * R, R), bf16),
            pltpu.VMEM((3 * nleaf, R, W), f32),
            pltpu.VMEM((6 * nleaf, W), f32),
            pltpu.VMEM((npair * R, R), f32),
            pltpu.VMEM((R, R, npair), bf16),
            pltpu.SMEM((2, 8, W), jnp.int32),
            pltpu.VMEM((2, 8, W), jnp.int32),
            pltpu.SemaphoreType.DMA,
            pltpu.SemaphoreType.DMA((4,)),
        ],
        compiler_params=pltpu.CompilerParams(vmem_limit_bytes=LIMIT),
        cost_estimate=pl.CostEstimate(flops=10**8, bytes_accessed=10**7, transcendentals=0),
        name="pairs",
    )(rows, cols, offs, packet, first, second)
    return jnp.transpose(out, (2, 0, 1))


LEAF = ("y", "z", "core")


def width(axes):
    return lax.axis_size(axes).bit_length() - 1


def swap(block, axes):
    return lax.all_to_all(block, axes, 0, 0)


def body(
    leaf_bases,
    local_transfer,
    path_transfer,
    leaf_points,
    pair_rows,
    pair_cols,
    pair_offsets,
    send_slots,
    send_counts,
):
    path = path_transfer[0, 0]
    points = leaf_points[0, 0]
    groups = [("core", "sub"), ("z",), ("y",)]
    sizes = [width(axes) for axes in groups]
    grams, mine, own = tree(leaf_bases[0, 0], local_transfer[0, 0], path, groups[0], sizes[0])
    factors, packet = local_chol(send_slots[0], send_counts, grams, points)

    count = lax.axis_size(LEAF)
    inside = [(i, i ^ 1) for i in range(count)]
    across = []
    for i in range(1, count - 1, 2):
        across += [(i, i + 1), (i + 1, i)]
    first = lax.ppermute(packet, LEAF, inside)
    second = lax.ppermute(packet, LEAF, across)

    level_grams = []
    base = 0
    for g in range(2):
        received = swap(mine, groups[g])
        done, mine, own = group_step(
            groups[g], sizes[g], base, groups[g + 1], sizes[g + 1], received, own, path
        )
        level_grams.append(done)
        base += sizes[g]
    received = swap(mine, groups[2])
    path_factors = path_chol(groups[2], sizes[2], base, received, own, path, level_grams)

    couplings = pairs(
        pair_rows[0], pair_cols[0], pair_offsets[0, 0], packet, first, second, points.shape[0]
    )
    return (factors[None, None], path_factors[None, None], couplings[None, None])


def solution(mesh):
    leaves, subs = mesh.devices.shape
    rows = 4 if leaves % 64 == 0 else 2
    parts = Mesh(mesh.devices.reshape(rows, leaves // rows // 2, 2, subs), LEAF + ("sub",))
    wide = P(LEAF, "sub", None, None, None)
    in_specs = (
        wide,
        wide,
        wide,
        wide,
        P(LEAF, "sub", None),
        P(LEAF, "sub", None),
        P(LEAF, "sub", None, None),
        P(LEAF, "sub", None),
        P(LEAF, "sub"),
    )
    return jax.shard_map(body, mesh=parts, in_specs=in_specs, out_specs=(wide, wide, wide), check_vma=False)
```

```python
import functools

import jax
import jax.numpy as jnp
from jax import lax
from jax.experimental import pallas as pl
from jax.experimental.pallas import tpu as pltpu
from jax.sharding import Mesh
from jax.sharding import PartitionSpec as P

R = 64
W = 2 * R
f32 = jnp.float32
bf16 = jnp.bfloat16
HIGH = lax.Precision.HIGH
VM = pl.BlockSpec(memory_space=pltpu.VMEM)
HB = pl.BlockSpec(memory_space=pltpu.HBM)
SM = pl.BlockSpec(memory_space=pltpu.SMEM)
LIMIT = 48 * 2**20
TREE_LIMIT = 48 * 2**20


def mm(a, b):
    return jnp.dot(a, b, precision=HIGH, preferred_element_type=f32)


def mm_t(a, b):
    dims = (((0,), (0,)), ((), ()))
    return lax.dot_general(a, b, dims, precision=HIGH, preferred_element_type=f32)


def carry(g, e):
    return mm_t(e, mm(g, e))


def pack(x):
    return jnp.concatenate([x[: R // 2], x[R // 2 :]], axis=1)


def unpack(x):
    return jnp.concatenate([x[:, :R], x[:, R:]], axis=0)


def products(transfers):
    out = [transfers[0]]
    for f in transfers[1:]:
        out.append(mm(out[-1], f))
    return out


def send(levels, me, h, transfers, K, s_ref):
    for i, f in enumerate(products(transfers)):
        K[i] = pack(carry(h, f))
    for p in range(2**levels):
        apart = me ^ p
        meet = jnp.int32(0)
        for i in range(1, levels):
            meet = meet + (apart >= 2**i).astype(jnp.int32)
        s_ref[p] = K[meet]
    return K[0]


def receive(levels, me, own, r_ref, transfers):
    sums = []
    for i in range(levels):
        first = ((me >> i) ^ 1) << i
        s = own + r_ref[first] if i == 0 else r_ref[first]
        for t in range(1, 2**i):
            s = s + r_ref[first + t]
        sums.append(unpack(s))
    grams = list(sums)
    for i in range(levels - 1):
        for j, f in enumerate(products(transfers[i + 1 :])):
            grams[i + 1 + j] = grams[i + 1 + j] + carry(sums[i], f)
    return grams


def tree_kernel(nleaf, axes, levels, b_hbm, e_hbm, p_hbm, g_ref, s_ref, own_ref, B, E, F, K, sem):
    copies = [
        pltpu.make_async_copy(b_hbm, B, sem.at[0]),
        pltpu.make_async_copy(e_hbm.at[pl.ds(0, nleaf)], E.at[pl.ds(0, nleaf)], sem.at[1]),
        pltpu.make_async_copy(e_hbm.at[pl.ds(nleaf, nleaf - 2)], E.at[pl.ds(nleaf, nleaf - 2)], sem.at[2]),
        pltpu.make_async_copy(p_hbm.at[pl.ds(0, levels)], F, sem.at[3]),
    ]
    for copy in copies:
        copy.start()
    copies[0].wait()
    held = [B[n] for n in range(nleaf)]
    out = [mm_t(b, b) for b in held]
    for n in range(nleaf):
        g_ref[n] = out[n]
    copies[1].wait()
    off, cnt = 0, nleaf
    while cnt > 1:
        if off == nleaf:
            copies[2].wait()
            copies[3].wait()
        nxt = off + cnt
        held = [(g_ref[off + n], E[off + n]) for n in range(cnt)]
        out = [carry(g, e) for g, e in held]
        for n in range(cnt // 2):
            g_ref[nxt + n] = out[2 * n] + out[2 * n + 1]
        off, cnt = nxt, cnt // 2
    root = g_ref[off]
    g_ref[off + 1] = root
    own_ref[...] = send(levels, lax.axis_index(axes), root, [F[i] for i in range(levels)], K, s_ref)


def tree(bases, transfers, path, axes, levels):
    n = bases.shape[0]
    return pl.pallas_call(
        functools.partial(tree_kernel, n, axes, levels),
        out_shape=(
            jax.ShapeDtypeStruct((2 * n, R, R), f32),
            jax.ShapeDtypeStruct((2**levels, R // 2, W), f32),
            jax.ShapeDtypeStruct((R // 2, W), f32),
        ),
        in_specs=[HB, HB, HB],
        out_specs=(VM, VM, VM),
        scratch_shapes=[
            pltpu.VMEM((n, R, R), f32),
            pltpu.VMEM((2 * n - 2, R, R), f32),
            pltpu.VMEM((levels, R, R), f32),
            pltpu.VMEM((levels, R // 2, W), f32),
            pltpu.SemaphoreType.DMA((4,)),
        ],
        compiler_params=pltpu.CompilerParams(vmem_limit_bytes=TREE_LIMIT),
        cost_estimate=pl.CostEstimate(flops=10**8, bytes_accessed=10**7, transcendentals=0),
        name="tree",
    )(bases, transfers, path)


def chol_core(T, lanes, blk=4):
    for b in range(R // blk):
        k0 = b * blk
        j0 = (k0 // 8) * 8
        n = R - j0
        acc = [T[pl.ds((k0 + r) * R + j0, n), :] for r in range(blk)]
        if k0 > 0:

            def step(i, acc, k0=k0, j0=j0, n=n):
                base = pl.multiple_of(i * R, R)
                row = T[pl.ds(base + j0, n), :]
                return tuple(acc[r] - T[pl.ds(base + k0 + r, 1), :] * row for r in range(blk))

            acc = list(lax.fori_loop(0, k0, step, tuple(acc), unroll=4))
        col = lax.broadcasted_iota(jnp.int32, (n, lanes), 0) + j0
        for r in range(blk):
            k = k0 + r
            row = acc[r] * lax.rsqrt(acc[r][k - j0 : k - j0 + 1, :])
            row = jnp.where(col >= k, row, 0.0)
            T[pl.ds(k * R + j0, n), :] = row
            if j0 > 0:
                T[pl.ds(k * R, j0), :] = jnp.zeros((j0, lanes), f32)
            for r2 in range(r + 1, blk):
                s = row[k0 + r2 - j0 : k0 + r2 - j0 + 1, :]
                acc[r2] = acc[r2] - s * row


def local_chol_kernel(nleaf, nb, slots, count, g_ref, p_ref, o_ref, k_ref, T, PT):
    lanes = nb + 1
    for i in range(R):
        T[pl.ds(i * R, R), :] = g_ref[pl.ds(i, lanes, stride=R), :].T
    chol_core(T, lanes)
    for i in range(R):
        o_ref[pl.ds(i, nb, stride=R), :] = T[pl.ds(i * R, R), :].T[:nb]
    half = nleaf // 2

    def put(n, _):
        at = pl.multiple_of(n * R, R)
        k_ref[pl.ds(at, R), :] = jnp.concatenate(
            [o_ref[pl.ds(at, R), :], o_ref[pl.ds(at + half * R, R), :]], axis=1
        )
        return _

    lax.fori_loop(0, half, put, 0, unroll=4)
    for r in range(nleaf):
        PT[3 * r : 3 * r + 3, :] = p_ref[r]
    points = 3 * half
    k_ref[half * R : half * R + points, :] = jnp.concatenate([PT[:points], PT[points:]], axis=1)
    lane = lax.broadcasted_iota(jnp.int32, (8, W), 1)
    chosen = jnp.zeros((8, W), f32)
    live = count[0, 0]
    nslot = slots.shape[1]
    for s in range(nslot):
        leaf = slots[0, jnp.minimum(s, live - 1)]
        chosen = jnp.where(lane == s, leaf.astype(f32), chosen)
    k_ref[half * R + points : half * R + points + 8, :] = chosen


def local_chol(slots, count, grams, points):
    nb = grams.shape[0] - 1
    nleaf = points.shape[0]
    rows = nleaf // 2 * R + 3 * nleaf // 2 + 8
    out, packet = pl.pallas_call(
        functools.partial(local_chol_kernel, nleaf, nb),
        out_shape=(
            jax.ShapeDtypeStruct((nb * R, R), f32),
            jax.ShapeDtypeStruct((rows, W), f32),
        ),
        in_specs=[SM, SM, VM, VM],
        out_specs=(VM, VM),
        scratch_shapes=[pltpu.VMEM((R * R, nb + 1), f32), pltpu.VMEM((3 * nleaf, R), f32)],
        compiler_params=pltpu.CompilerParams(vmem_limit_bytes=LIMIT),
        cost_estimate=pl.CostEstimate(flops=10**8, bytes_accessed=10**7, transcendentals=0),
        name="local_chol",
    )(slots, count, grams.reshape((nb + 1) * R, R), points)
    return out.reshape(nb, R, R), packet


def group_kernel(axes, levels, base, axes2, levels2, r_ref, own_ref, e_ref, h_ref, s_ref, next_ref, K):
    fs = [e_ref[base + i] for i in range(levels + levels2)]
    grams = receive(levels, lax.axis_index(axes), own_ref[...], r_ref, fs[:levels])
    for i in range(levels):
        h_ref[i] = grams[i]
    next_ref[...] = send(levels2, lax.axis_index(axes2), grams[-1], fs[levels:], K, s_ref)


def group_step(axes, levels, base, axes2, levels2, received, own, path):
    return pl.pallas_call(
        functools.partial(group_kernel, axes, levels, base, axes2, levels2),
        out_shape=(
            jax.ShapeDtypeStruct((levels, R, R), f32),
            jax.ShapeDtypeStruct((2**levels2, R // 2, W), f32),
            jax.ShapeDtypeStruct((R // 2, W), f32),
        ),
        in_specs=[VM, VM, VM],
        out_specs=(VM, VM, VM),
        scratch_shapes=[pltpu.VMEM((levels2, R // 2, W), f32)],
        cost_estimate=pl.CostEstimate(flops=10**7, bytes_accessed=10**6, transcendentals=0),
        name="group_step",
    )(received, own, path)


def path_chol_kernel(axes, levels, base, counts, *refs):
    r_ref, own_ref, e_ref = refs[:3]
    o_ref, T, S = refs[-3:]
    done = 0
    for count, ref in zip(counts, refs[3:-3]):
        for n in range(count):
            S[pl.ds((done + n) * R, R), :] = ref[n]
        done += count
    fs = [e_ref[base + i] for i in range(levels)]
    grams = receive(levels, lax.axis_index(axes), own_ref[...], r_ref, fs)
    total = done + levels
    lanes = S.shape[0] // R
    for n in range(done, lanes):
        S[pl.ds(n * R, R), :] = grams[min(n - done, levels - 1)]
    for i in range(R):
        T[pl.ds(i * R, R), :] = S[pl.ds(i, lanes, stride=R), :].T
    chol_core(T, lanes)
    for i in range(R):
        o_ref[pl.ds(i, total, stride=R), :] = T[pl.ds(i * R, R), :].T[:total]


def path_chol(axes, levels, base, received, own, path, grams):
    counts = [g.shape[0] for g in grams]
    total = sum(counts) + levels
    lanes = (total + 7) // 8 * 8
    out = pl.pallas_call(
        functools.partial(path_chol_kernel, axes, levels, base, counts),
        out_shape=jax.ShapeDtypeStruct((total * R, R), f32),
        in_specs=[VM] * (3 + len(grams)),
        out_specs=VM,
        scratch_shapes=[pltpu.VMEM((R * R, lanes), f32), pltpu.VMEM((lanes * R, R), f32)],
        compiler_params=pltpu.CompilerParams(vmem_limit_bytes=LIMIT),
        cost_estimate=pl.CostEstimate(flops=10**7, bytes_accessed=10**6, transcendentals=0),
        name="path_chol",
    )(received, own, path, *grams)
    return out.reshape(total, R, R)


def pairs_kernel(
    nleaf, npair, rows, cols, offs, k_ref, a_ref, b_ref, o_hbm, RF, CF, PB, Q, S, OT, table, spot, sem, out_sem
):
    half = nleaf // 2
    points = 3 * half
    mark = half * R + points
    for side, r_ref in enumerate((a_ref, b_ref)):
        spot[side] = r_ref[mark : mark + 8, :].astype(jnp.int32)
    copy = pltpu.make_async_copy(spot, table, sem)
    copy.start()

    def prep_row(n, _):
        both = k_ref[pl.ds(pl.multiple_of(n * R, R), R), :]
        RF[n] = both[:, :R]
        RF[half + n] = both[:, R:]
        return _

    lax.fori_loop(0, half, prep_row, 0, unroll=4)
    pt = k_ref[half * R : mark, :].T
    for r in range(points):
        PB[r] = jnp.broadcast_to(pt[:R, r : r + 1], (R, R))
        PB[points + r] = jnp.broadcast_to(pt[R:, r : r + 1], (R, R))
    for side, r_ref in enumerate((a_ref, b_ref)):

        def prep_col(n, _, side=side, r_ref=r_ref):
            both = r_ref[pl.ds(pl.multiple_of(n * R, R), R), :].T
            CF[side * nleaf + n] = both[:R]
            CF[side * nleaf + half + n] = both[R:]
            return _

        lax.fori_loop(0, half, prep_col, 0, unroll=4)
        q = r_ref[half * R : mark, :]
        Q[side * 2 * points : side * 2 * points + points, :] = q[:, :R]
        Q[side * 2 * points + points : (side + 1) * 2 * points, :] = q[:, R:]
    copy.wait()
    odd = lax.axis_index("core")
    wide = 16

    def block(t, _):
        ks = [t * wide + u for u in range(wide)]
        rs = [rows[0, k] for k in ks]
        cs = []
        for k in ks:
            v = cols[0, k]
            right = v // nleaf
            side = jnp.where(odd == 1, right, 1 - right)
            cs.append(side * nleaf + table[side, 0, v % nleaf])
        near = []
        for k, r, c in zip(ks, rs, cs):
            d2 = None
            for a in range(3):
                q = Q[pl.ds(3 * c + a, 1), :] + offs[a, k].astype(f32)
                d = PB[3 * r + a] - q
                d2 = d * d if d2 is None else d2 + d * d
            near.append(lax.rsqrt(d2))
        left = [mm(x, CF[c]) for x, c in zip(near, cs)]
        out = [mm(RF[r], x) for x, r in zip(left, rs)]
        for u in range(wide):
            S[pl.ds(pl.multiple_of(ks[u] * R, R), R), :] = out[u]
        return _

    lax.fori_loop(0, npair // wide, block, 0)
    parts = 4
    rows_each = R // parts
    copies = []
    for c in range(parts):
        for i in range(c * rows_each, (c + 1) * rows_each):
            OT[i] = S[pl.ds(i, npair, stride=R), :].T.astype(bf16)
        at = pl.ds(c * rows_each, rows_each)
        copies.append(pltpu.make_async_copy(OT.at[at], o_hbm.at[at], out_sem.at[c]))
        copies[-1].start()
    for copy in copies:
        copy.wait()


def pairs(rows, cols, offs, packet, first, second, nleaf):
    npair = rows.shape[1]
    out = pl.pallas_call(
        functools.partial(pairs_kernel, nleaf, npair),
        out_shape=jax.ShapeDtypeStruct((R, R, npair), bf16),
        in_specs=[SM, SM, SM, VM, VM, VM],
        out_specs=HB,
        scratch_shapes=[
            pltpu.VMEM((nleaf, R, R), f32),
            pltpu.VMEM((2 * nleaf, R, R), f32),
            pltpu.VMEM((3 * nleaf, R, R), f32),
            pltpu.VMEM((6 * nleaf, R), f32),
            pltpu.VMEM((npair * R, R), f32),
            pltpu.VMEM((R, R, npair), bf16),
            pltpu.SMEM((2, 8, W), jnp.int32),
            pltpu.VMEM((2, 8, W), jnp.int32),
            pltpu.SemaphoreType.DMA,
            pltpu.SemaphoreType.DMA((4,)),
        ],
        compiler_params=pltpu.CompilerParams(vmem_limit_bytes=LIMIT),
        cost_estimate=pl.CostEstimate(flops=10**8, bytes_accessed=10**7, transcendentals=0),
        name="pairs",
    )(rows, cols, offs, packet, first, second)
    return jnp.transpose(out, (2, 0, 1))


LEAF = ("y", "z", "core")


def width(axes):
    return lax.axis_size(axes).bit_length() - 1


def swap(block, axes):
    return lax.all_to_all(block, axes, 0, 0)


def body(
    leaf_bases,
    local_transfer,
    path_transfer,
    leaf_points,
    pair_rows,
    pair_cols,
    pair_offsets,
    send_slots,
    send_counts,
):
    path = path_transfer[0, 0]
    points = leaf_points[0, 0]
    groups = [("core", "sub"), ("z",), ("y",)]
    sizes = [width(axes) for axes in groups]
    grams, mine, own = tree(leaf_bases[0, 0], local_transfer[0, 0], path, groups[0], sizes[0])
    factors, packet = local_chol(send_slots[0], send_counts, grams, points)

    level_grams = []
    base = 0
    for g in range(2):
        received = swap(mine, groups[g])
        if g == 0:
            received, packet, factors = lax.optimization_barrier((received, packet, factors))
        done, mine, own = group_step(
            groups[g], sizes[g], base, groups[g + 1], sizes[g + 1], received, own, path
        )
        if g == 0:
            mine, packet = lax.optimization_barrier((mine, packet))
        level_grams.append(done)
        base += sizes[g]
    count = lax.axis_size(LEAF)
    inside = [(i, i ^ 1) for i in range(count)]
    across = []
    for i in range(1, count - 1, 2):
        across += [(i, i + 1), (i + 1, i)]
    first = lax.ppermute(packet, LEAF, inside)
    second = lax.ppermute(packet, LEAF, across)
    received = swap(mine, groups[2])
    path_factors = path_chol(groups[2], sizes[2], base, received, own, path, level_grams)

    couplings = pairs(
        pair_rows[0], pair_cols[0], pair_offsets[0, 0], packet, first, second, points.shape[0]
    )
    return (factors[None, None], path_factors[None, None], couplings[None, None])


def solution(mesh):
    leaves, subs = mesh.devices.shape
    rows = 4 if leaves % 64 == 0 else 2
    parts = Mesh(mesh.devices.reshape(rows, leaves // rows // 2, 2, subs), LEAF + ("sub",))
    wide = P(LEAF, "sub", None, None, None)
    in_specs = (
        wide,
        wide,
        wide,
        wide,
        P(LEAF, "sub", None),
        P(LEAF, "sub", None),
        P(LEAF, "sub", None, None),
        P(LEAF, "sub", None),
        P(LEAF, "sub"),
    )
    return jax.shard_map(body, mesh=parts, in_specs=in_specs, out_specs=(wide, wide, wide), check_vma=False)
```

```python
import functools

import jax
import jax.numpy as jnp
from jax import lax
from jax.experimental import pallas as pl
from jax.experimental.pallas import tpu as pltpu
from jax.sharding import Mesh
from jax.sharding import PartitionSpec as P

R = 64
W = 2 * R
f32 = jnp.float32
bf16 = jnp.bfloat16
HIGH = lax.Precision.HIGH
VM = pl.BlockSpec(memory_space=pltpu.VMEM)
HB = pl.BlockSpec(memory_space=pltpu.HBM)
SM = pl.BlockSpec(memory_space=pltpu.SMEM)
LIMIT = 48 * 2**20
FULL = 60 * 2**20


def mm(a, b):
    return jnp.dot(a, b, precision=HIGH, preferred_element_type=f32)


def mm_t(a, b):
    dims = (((0,), (0,)), ((), ()))
    return lax.dot_general(a, b, dims, precision=HIGH, preferred_element_type=f32)


def carry(g, e):
    return mm_t(e, mm(g, e))


def pack(x):
    return jnp.concatenate([x[: R // 2], x[R // 2 :]], axis=1)


def unpack(x):
    return jnp.concatenate([x[:, :R], x[:, R:]], axis=0)


def products(transfers):
    out = [transfers[0]]
    for f in transfers[1:]:
        out.append(mm(out[-1], f))
    return out


def send(levels, me, h, transfers, K, s_ref):
    for i, f in enumerate(products(transfers)):
        K[i] = pack(carry(h, f))
    for p in range(2**levels):
        apart = me ^ p
        meet = jnp.int32(0)
        for i in range(1, levels):
            meet = meet + (apart >= 2**i).astype(jnp.int32)
        s_ref[p] = K[meet]
    return K[0]


def receive(levels, me, own, r_ref, transfers):
    sums = []
    for i in range(levels):
        first = ((me >> i) ^ 1) << i
        s = own + r_ref[first] if i == 0 else r_ref[first]
        for t in range(1, 2**i):
            s = s + r_ref[first + t]
        sums.append(unpack(s))
    grams = list(sums)
    for i in range(levels - 1):
        for j, f in enumerate(products(transfers[i + 1 :])):
            grams[i + 1 + j] = grams[i + 1 + j] + carry(sums[i], f)
    return grams


def tree_kernel(nleaf, axes, levels, b_hbm, e_hbm, p_hbm, g_hbm, s_ref, own_ref, G, B, E, F, K, sem, out_sem):
    chunk = nleaf // 4
    bases = [
        pltpu.make_async_copy(b_hbm.at[pl.ds(c * chunk, chunk)], B.at[pl.ds(c * chunk, chunk)], sem.at[c])
        for c in range(4)
    ]
    copies = [
        pltpu.make_async_copy(e_hbm.at[pl.ds(0, nleaf)], E.at[pl.ds(0, nleaf)], sem.at[4]),
        pltpu.make_async_copy(e_hbm.at[pl.ds(nleaf, nleaf - 2)], E.at[pl.ds(nleaf, nleaf - 2)], sem.at[5]),
        pltpu.make_async_copy(p_hbm.at[pl.ds(0, levels)], F, sem.at[6]),
    ]
    for copy in bases + copies:
        copy.start()
    for c in range(4):
        bases[c].wait()
        held = [B[c * chunk + n] for n in range(chunk)]
        out = [mm_t(b, b) for b in held]
        for n in range(chunk):
            G[c * chunk + n] = out[n]
    sent = [pltpu.make_async_copy(G.at[pl.ds(0, nleaf)], g_hbm.at[pl.ds(0, nleaf)], out_sem.at[0])]
    sent[0].start()
    copies[0].wait()
    off, cnt = 0, nleaf
    while cnt > 1:
        if off == nleaf:
            copies[1].wait()
            copies[2].wait()
        nxt = off + cnt
        held = [(G[off + n], E[off + n]) for n in range(cnt)]
        out = [carry(g, e) for g, e in held]
        for n in range(cnt // 2):
            G[nxt + n] = out[2 * n] + out[2 * n + 1]
        off, cnt = nxt, cnt // 2
        if off == nleaf:
            at = pl.ds(nleaf, cnt)
            sent.append(pltpu.make_async_copy(G.at[at], g_hbm.at[at], out_sem.at[1]))
            sent[1].start()
    root = G[off]
    G[off + 1] = root
    at = pl.ds(nleaf + nleaf // 2, nleaf // 2)
    sent.append(pltpu.make_async_copy(G.at[at], g_hbm.at[at], out_sem.at[2]))
    sent[2].start()
    own_ref[...] = send(levels, lax.axis_index(axes), root, [F[i] for i in range(levels)], K, s_ref)
    for copy in sent:
        copy.wait()


def tree(bases, transfers, path, axes, levels):
    n = bases.shape[0]
    return pl.pallas_call(
        functools.partial(tree_kernel, n, axes, levels),
        out_shape=(
            jax.ShapeDtypeStruct((2 * n, R, R), f32),
            jax.ShapeDtypeStruct((2**levels, R // 2, W), f32),
            jax.ShapeDtypeStruct((R // 2, W), f32),
        ),
        in_specs=[HB, HB, HB],
        out_specs=(HB, VM, VM),
        scratch_shapes=[
            pltpu.VMEM((2 * n, R, R), f32),
            pltpu.VMEM((n, R, R), f32),
            pltpu.VMEM((2 * n - 2, R, R), f32),
            pltpu.VMEM((levels, R, R), f32),
            pltpu.VMEM((levels, R // 2, W), f32),
            pltpu.SemaphoreType.DMA((7,)),
            pltpu.SemaphoreType.DMA((3,)),
        ],
        compiler_params=pltpu.CompilerParams(vmem_limit_bytes=FULL),
        cost_estimate=pl.CostEstimate(flops=10**8, bytes_accessed=10**7, transcendentals=0),
        name="tree",
    )(bases, transfers, path)


def chol_core(T, lanes, blk=4):
    for b in range(R // blk):
        k0 = b * blk
        j0 = (k0 // 8) * 8
        n = R - j0
        acc = [T[pl.ds((k0 + r) * R + j0, n), :] for r in range(blk)]
        if k0 > 0:

            def step(i, acc, k0=k0, j0=j0, n=n):
                base = pl.multiple_of(i * R, R)
                row = T[pl.ds(base + j0, n), :]
                return tuple(acc[r] - T[pl.ds(base + k0 + r, 1), :] * row for r in range(blk))

            acc = list(lax.fori_loop(0, k0, step, tuple(acc), unroll=4))
        col = lax.broadcasted_iota(jnp.int32, (n, lanes), 0) + j0
        for r in range(blk):
            k = k0 + r
            row = acc[r] * lax.rsqrt(acc[r][k - j0 : k - j0 + 1, :])
            row = jnp.where(col >= k, row, 0.0)
            T[pl.ds(k * R + j0, n), :] = row
            if j0 > 0:
                T[pl.ds(k * R, j0), :] = jnp.zeros((j0, lanes), f32)
            for r2 in range(r + 1, blk):
                s = row[k0 + r2 - j0 : k0 + r2 - j0 + 1, :]
                acc[r2] = acc[r2] - s * row


def local_chol_kernel(nleaf, nb, slots, count, g_ref, p_ref, o_ref, k_ref, T, PT):
    lanes = nb + 1
    for i in range(R):
        T[pl.ds(i * R, R), :] = g_ref[pl.ds(i, lanes, stride=R), :].T
    chol_core(T, lanes)
    for i in range(R):
        o_ref[pl.ds(i, nb, stride=R), :] = T[pl.ds(i * R, R), :].T[:nb]
    half = nleaf // 2

    def put(n, _):
        at = pl.multiple_of(n * R, R)
        k_ref[pl.ds(at, R), :] = jnp.concatenate(
            [o_ref[pl.ds(at, R), :], o_ref[pl.ds(at + half * R, R), :]], axis=1
        )
        return _

    lax.fori_loop(0, half, put, 0, unroll=4)
    for r in range(nleaf):
        PT[3 * r : 3 * r + 3, :] = p_ref[r]
    points = 3 * half
    k_ref[half * R : half * R + points, :] = jnp.concatenate([PT[:points], PT[points:]], axis=1)
    lane = lax.broadcasted_iota(jnp.int32, (8, W), 1)
    chosen = jnp.zeros((8, W), f32)
    live = count[0, 0]
    nslot = slots.shape[1]
    for s in range(nslot):
        leaf = slots[0, jnp.minimum(s, live - 1)]
        chosen = jnp.where(lane == s, leaf.astype(f32), chosen)
    k_ref[half * R + points : half * R + points + 8, :] = chosen


def local_chol(slots, count, grams, points):
    nb = grams.shape[0] - 1
    nleaf = points.shape[0]
    rows = nleaf // 2 * R + 3 * nleaf // 2 + 8
    out, packet = pl.pallas_call(
        functools.partial(local_chol_kernel, nleaf, nb),
        out_shape=(
            jax.ShapeDtypeStruct((nb * R, R), f32),
            jax.ShapeDtypeStruct((rows, W), f32),
        ),
        in_specs=[SM, SM, VM, VM],
        out_specs=(VM, VM),
        scratch_shapes=[pltpu.VMEM((R * R, nb + 1), f32), pltpu.VMEM((3 * nleaf, R), f32)],
        compiler_params=pltpu.CompilerParams(vmem_limit_bytes=FULL),
        cost_estimate=pl.CostEstimate(flops=10**8, bytes_accessed=10**7, transcendentals=0),
        name="local_chol",
    )(slots, count, grams.reshape((nb + 1) * R, R), points)
    return out.reshape(nb, R, R), packet


def group_kernel(axes, levels, base, axes2, levels2, r_ref, own_ref, e_ref, h_ref, s_ref, next_ref, K):
    fs = [e_ref[base + i] for i in range(levels + levels2)]
    grams = receive(levels, lax.axis_index(axes), own_ref[...], r_ref, fs[:levels])
    for i in range(levels):
        h_ref[i] = grams[i]
    next_ref[...] = send(levels2, lax.axis_index(axes2), grams[-1], fs[levels:], K, s_ref)


def group_step(axes, levels, base, axes2, levels2, received, own, path):
    return pl.pallas_call(
        functools.partial(group_kernel, axes, levels, base, axes2, levels2),
        out_shape=(
            jax.ShapeDtypeStruct((levels, R, R), f32),
            jax.ShapeDtypeStruct((2**levels2, R // 2, W), f32),
            jax.ShapeDtypeStruct((R // 2, W), f32),
        ),
        in_specs=[VM, VM, VM],
        out_specs=(VM, VM, VM),
        scratch_shapes=[pltpu.VMEM((levels2, R // 2, W), f32)],
        compiler_params=pltpu.CompilerParams(vmem_limit_bytes=16 * 2**20),
        cost_estimate=pl.CostEstimate(flops=10**7, bytes_accessed=10**6, transcendentals=0),
        name="group_step",
    )(received, own, path)


def path_chol_kernel(axes, levels, base, counts, *refs):
    r_ref, own_ref, e_ref = refs[:3]
    o_ref, T, S = refs[-3:]
    done = 0
    for count, ref in zip(counts, refs[3:-3]):
        for n in range(count):
            S[pl.ds((done + n) * R, R), :] = ref[n]
        done += count
    fs = [e_ref[base + i] for i in range(levels)]
    grams = receive(levels, lax.axis_index(axes), own_ref[...], r_ref, fs)
    total = done + levels
    lanes = S.shape[0] // R
    for n in range(done, lanes):
        S[pl.ds(n * R, R), :] = grams[min(n - done, levels - 1)]
    for i in range(R):
        T[pl.ds(i * R, R), :] = S[pl.ds(i, lanes, stride=R), :].T
    chol_core(T, lanes)
    for i in range(R):
        o_ref[pl.ds(i, total, stride=R), :] = T[pl.ds(i * R, R), :].T[:total]


def path_chol(axes, levels, base, received, own, path, grams):
    counts = [g.shape[0] for g in grams]
    total = sum(counts) + levels
    lanes = (total + 7) // 8 * 8
    out = pl.pallas_call(
        functools.partial(path_chol_kernel, axes, levels, base, counts),
        out_shape=jax.ShapeDtypeStruct((total * R, R), f32),
        in_specs=[VM] * (3 + len(grams)),
        out_specs=VM,
        scratch_shapes=[pltpu.VMEM((R * R, lanes), f32), pltpu.VMEM((lanes * R, R), f32)],
        compiler_params=pltpu.CompilerParams(vmem_limit_bytes=LIMIT),
        cost_estimate=pl.CostEstimate(flops=10**7, bytes_accessed=10**6, transcendentals=0),
        name="path_chol",
    )(received, own, path, *grams)
    return out.reshape(total, R, R)


def pairs_kernel(
    nleaf, npair, rows, cols, offs, k_ref, a_ref, b_ref, o_hbm, RF, CF, PB, Q, S, OT, table, spot, sem, out_sem
):
    half = nleaf // 2
    points = 3 * half
    mark = half * R + points
    for side, r_ref in enumerate((a_ref, b_ref)):
        spot[side] = r_ref[mark : mark + 8, :].astype(jnp.int32)
    copy = pltpu.make_async_copy(spot, table, sem)
    copy.start()

    def prep_row(n, _):
        both = k_ref[pl.ds(pl.multiple_of(n * R, R), R), :]
        RF[n] = both[:, :R]
        RF[half + n] = both[:, R:]
        return _

    lax.fori_loop(0, half, prep_row, 0, unroll=4)
    pt = k_ref[half * R : mark, :].T
    for r in range(points):
        PB[r] = jnp.broadcast_to(pt[:R, r : r + 1], (R, R))
        PB[points + r] = jnp.broadcast_to(pt[R:, r : r + 1], (R, R))
    for side, r_ref in enumerate((a_ref, b_ref)):

        def prep_col(n, _, side=side, r_ref=r_ref):
            both = r_ref[pl.ds(pl.multiple_of(n * R, R), R), :].T
            CF[side * nleaf + n] = both[:R]
            CF[side * nleaf + half + n] = both[R:]
            return _

        lax.fori_loop(0, half, prep_col, 0, unroll=4)
        q = r_ref[half * R : mark, :]
        Q[side * 2 * points : side * 2 * points + points, :] = q[:, :R]
        Q[side * 2 * points + points : (side + 1) * 2 * points, :] = q[:, R:]
    copy.wait()
    odd = lax.axis_index("core")
    wide = 16

    def block(t, _):
        ks = [t * wide + u for u in range(wide)]
        rs = [rows[0, k] for k in ks]
        cs = []
        for k in ks:
            v = cols[0, k]
            right = v // nleaf
            side = jnp.where(odd == 1, right, 1 - right)
            cs.append(side * nleaf + table[side, 0, v % nleaf])
        near = []
        for k, r, c in zip(ks, rs, cs):
            d2 = None
            for a in range(3):
                q = Q[pl.ds(3 * c + a, 1), :] + offs[a, k].astype(f32)
                d = PB[3 * r + a] - q
                d2 = d * d if d2 is None else d2 + d * d
            near.append(lax.rsqrt(d2))
        left = [mm(x, CF[c]) for x, c in zip(near, cs)]
        out = [mm(RF[r], x) for x, r in zip(left, rs)]
        for u in range(wide):
            S[pl.ds(pl.multiple_of(ks[u] * R, R), R), :] = out[u]
        return _

    lax.fori_loop(0, npair // wide, block, 0)
    parts = 4
    rows_each = R // parts
    copies = []
    for c in range(parts):
        for i in range(c * rows_each, (c + 1) * rows_each):
            OT[i] = S[pl.ds(i, npair, stride=R), :].T.astype(bf16)
        at = pl.ds(c * rows_each, rows_each)
        copies.append(pltpu.make_async_copy(OT.at[at], o_hbm.at[at], out_sem.at[c]))
        copies[-1].start()
    for copy in copies:
        copy.wait()


def pairs(rows, cols, offs, packet, first, second, nleaf):
    npair = rows.shape[1]
    out = pl.pallas_call(
        functools.partial(pairs_kernel, nleaf, npair),
        out_shape=jax.ShapeDtypeStruct((R, R, npair), bf16),
        in_specs=[SM, SM, SM, VM, VM, VM],
        out_specs=HB,
        scratch_shapes=[
            pltpu.VMEM((nleaf, R, R), f32),
            pltpu.VMEM((2 * nleaf, R, R), f32),
            pltpu.VMEM((3 * nleaf, R, R), f32),
            pltpu.VMEM((6 * nleaf, R), f32),
            pltpu.VMEM((npair * R, R), f32),
            pltpu.VMEM((R, R, npair), bf16),
            pltpu.SMEM((2, 8, W), jnp.int32),
            pltpu.VMEM((2, 8, W), jnp.int32),
            pltpu.SemaphoreType.DMA,
            pltpu.SemaphoreType.DMA((4,)),
        ],
        compiler_params=pltpu.CompilerParams(vmem_limit_bytes=LIMIT),
        cost_estimate=pl.CostEstimate(flops=10**8, bytes_accessed=10**7, transcendentals=0),
        name="pairs",
    )(rows, cols, offs, packet, first, second)
    return jnp.transpose(out, (2, 0, 1))


LEAF = ("y", "zh", "zl", "core")


def width(axes):
    return lax.axis_size(axes).bit_length() - 1


def swap(block, axes):
    return lax.all_to_all(block, axes, 0, 0)


def body(
    leaf_bases,
    local_transfer,
    path_transfer,
    leaf_points,
    pair_rows,
    pair_cols,
    pair_offsets,
    send_slots,
    send_counts,
):
    path = path_transfer[0, 0]
    points = leaf_points[0, 0]
    groups = [("core", "sub"), ("zl",), ("zh",), ("y",)]
    sizes = [width(axes) for axes in groups]
    grams, mine, own = tree(leaf_bases[0, 0], local_transfer[0, 0], path, groups[0], sizes[0])
    factors, packet = local_chol(send_slots[0], send_counts, grams, points)

    level_grams = []
    base = 0
    for g in range(len(groups) - 1):
        received = swap(mine, groups[g])
        if g == 0:
            received, packet, factors = lax.optimization_barrier((received, packet, factors))
        done, mine, own = group_step(
            groups[g], sizes[g], base, groups[g + 1], sizes[g + 1], received, own, path
        )
        if g == 0:
            mine, packet = lax.optimization_barrier((mine, packet))
        level_grams.append(done)
        base += sizes[g]
    count = lax.axis_size(LEAF)
    inside = [(i, i ^ 1) for i in range(count)]
    across = []
    for i in range(1, count - 1, 2):
        across += [(i, i + 1), (i + 1, i)]
    first = lax.ppermute(packet, LEAF, inside)
    second = lax.ppermute(packet, LEAF, across)
    received = swap(mine, groups[-1])
    path_factors = path_chol(groups[-1], sizes[-1], base, received, own, path, level_grams)

    couplings = pairs(
        pair_rows[0], pair_cols[0], pair_offsets[0, 0], packet, first, second, points.shape[0]
    )
    return (factors[None, None], path_factors[None, None], couplings[None, None])


def solution(mesh):
    leaves, subs = mesh.devices.shape
    rows = 4 if leaves % 64 == 0 else 2
    near = 4 if leaves // rows >= 32 else 2
    far = leaves // rows // near // 2
    parts = Mesh(mesh.devices.reshape(rows, far, near, 2, subs), LEAF + ("sub",))
    wide = P(LEAF, "sub", None, None, None)
    in_specs = (
        wide,
        wide,
        wide,
        wide,
        P(LEAF, "sub", None),
        P(LEAF, "sub", None),
        P(LEAF, "sub", None, None),
        P(LEAF, "sub", None),
        P(LEAF, "sub"),
    )
    return jax.shard_map(body, mesh=parts, in_specs=in_specs, out_specs=(wide, wide, wide), check_vma=False)
```

```python
import functools

import jax
import jax.numpy as jnp
from jax import lax
from jax.experimental import pallas as pl
from jax.experimental.pallas import tpu as pltpu
from jax.sharding import Mesh
from jax.sharding import PartitionSpec as P

R = 64
W = 2 * R
f32 = jnp.float32
bf16 = jnp.bfloat16
HIGH = lax.Precision.HIGH
VM = pl.BlockSpec(memory_space=pltpu.VMEM)
HB = pl.BlockSpec(memory_space=pltpu.HBM)
SM = pl.BlockSpec(memory_space=pltpu.SMEM)
LIMIT = 48 * 2**20
FULL = 60 * 2**20


def mm(a, b):
    return jnp.dot(a, b, precision=HIGH, preferred_element_type=f32)


def mm_t(a, b):
    dims = (((0,), (0,)), ((), ()))
    return lax.dot_general(a, b, dims, precision=HIGH, preferred_element_type=f32)


def carry(g, e):
    return mm_t(e, mm(g, e))


def pack(x):
    return jnp.concatenate([x[: R // 2], x[R // 2 :]], axis=1)


def unpack(x):
    return jnp.concatenate([x[:, :R], x[:, R:]], axis=0)


def products(transfers):
    out = [transfers[0]]
    for f in transfers[1:]:
        out.append(mm(out[-1], f))
    return out


def send(levels, me, h, transfers, K, s_ref):
    for i, f in enumerate(products(transfers)):
        K[i] = pack(carry(h, f))
    for p in range(2**levels):
        apart = me ^ p
        meet = jnp.int32(0)
        for i in range(1, levels):
            meet = meet + (apart >= 2**i).astype(jnp.int32)
        s_ref[p] = K[meet]
    return K[0]


def receive(levels, me, own, r_ref, transfers):
    sums = []
    for i in range(levels):
        first = ((me >> i) ^ 1) << i
        s = own + r_ref[first] if i == 0 else r_ref[first]
        for t in range(1, 2**i):
            s = s + r_ref[first + t]
        sums.append(unpack(s))
    grams = list(sums)
    for i in range(levels - 1):
        for j, f in enumerate(products(transfers[i + 1 :])):
            grams[i + 1 + j] = grams[i + 1 + j] + carry(sums[i], f)
    return grams


def tree_kernel(nleaf, axes, levels, b_hbm, e_hbm, p_hbm, g_hbm, s_ref, own_ref, G, B, E, F, K, sem, out_sem):
    chunk = nleaf // 4
    bases = [
        pltpu.make_async_copy(b_hbm.at[pl.ds(c * chunk, chunk)], B.at[pl.ds(c * chunk, chunk)], sem.at[c])
        for c in range(4)
    ]
    copies = [
        pltpu.make_async_copy(e_hbm.at[pl.ds(0, nleaf)], E.at[pl.ds(0, nleaf)], sem.at[4]),
        pltpu.make_async_copy(e_hbm.at[pl.ds(nleaf, nleaf - 2)], E.at[pl.ds(nleaf, nleaf - 2)], sem.at[5]),
        pltpu.make_async_copy(p_hbm.at[pl.ds(0, levels)], F, sem.at[6]),
    ]
    for copy in bases + copies:
        copy.start()
    for c in range(4):
        bases[c].wait()
        held = [B[c * chunk + n] for n in range(chunk)]
        out = [mm_t(b, b) for b in held]
        for n in range(chunk):
            G[c * chunk + n] = out[n]
    sent = [pltpu.make_async_copy(G.at[pl.ds(0, nleaf)], g_hbm.at[pl.ds(0, nleaf)], out_sem.at[0])]
    sent[0].start()
    copies[0].wait()
    off, cnt = 0, nleaf
    while cnt > 1:
        if off == nleaf:
            copies[1].wait()
            copies[2].wait()
        nxt = off + cnt
        held = [(G[off + n], E[off + n]) for n in range(cnt)]
        out = [carry(g, e) for g, e in held]
        for n in range(cnt // 2):
            G[nxt + n] = out[2 * n] + out[2 * n + 1]
        off, cnt = nxt, cnt // 2
        if off == nleaf:
            at = pl.ds(nleaf, cnt)
            sent.append(pltpu.make_async_copy(G.at[at], g_hbm.at[at], out_sem.at[1]))
            sent[1].start()
    root = G[off]
    G[off + 1] = root
    at = pl.ds(nleaf + nleaf // 2, nleaf // 2)
    sent.append(pltpu.make_async_copy(G.at[at], g_hbm.at[at], out_sem.at[2]))
    sent[2].start()
    own_ref[...] = send(levels, lax.axis_index(axes), root, [F[i] for i in range(levels)], K, s_ref)
    for copy in sent:
        copy.wait()


def tree(bases, transfers, path, axes, levels):
    n = bases.shape[0]
    return pl.pallas_call(
        functools.partial(tree_kernel, n, axes, levels),
        out_shape=(
            jax.ShapeDtypeStruct((2 * n, R, R), f32),
            jax.ShapeDtypeStruct((2**levels, R // 2, W), f32),
            jax.ShapeDtypeStruct((R // 2, W), f32),
        ),
        in_specs=[HB, HB, HB],
        out_specs=(HB, VM, VM),
        scratch_shapes=[
            pltpu.VMEM((2 * n, R, R), f32),
            pltpu.VMEM((n, R, R), f32),
            pltpu.VMEM((2 * n - 2, R, R), f32),
            pltpu.VMEM((levels, R, R), f32),
            pltpu.VMEM((levels, R // 2, W), f32),
            pltpu.SemaphoreType.DMA((7,)),
            pltpu.SemaphoreType.DMA((3,)),
        ],
        compiler_params=pltpu.CompilerParams(vmem_limit_bytes=FULL),
        cost_estimate=pl.CostEstimate(flops=10**8, bytes_accessed=10**7, transcendentals=0),
        name="tree",
    )(bases, transfers, path)


def chol_core(T, lanes, blk=4):
    for b in range(R // blk):
        k0 = b * blk
        j0 = (k0 // 8) * 8
        n = R - j0
        acc = [T[pl.ds((k0 + r) * R + j0, n), :] for r in range(blk)]
        if k0 > 0:

            def step(i, acc, k0=k0, j0=j0, n=n):
                base = pl.multiple_of(i * R, R)
                row = T[pl.ds(base + j0, n), :]
                return tuple(acc[r] - T[pl.ds(base + k0 + r, 1), :] * row for r in range(blk))

            acc = list(lax.fori_loop(0, k0, step, tuple(acc), unroll=4))
        col = lax.broadcasted_iota(jnp.int32, (n, lanes), 0) + j0
        for r in range(blk):
            k = k0 + r
            row = acc[r] * lax.rsqrt(acc[r][k - j0 : k - j0 + 1, :])
            row = jnp.where(col >= k, row, 0.0)
            T[pl.ds(k * R + j0, n), :] = row
            if j0 > 0:
                T[pl.ds(k * R, j0), :] = jnp.zeros((j0, lanes), f32)
            for r2 in range(r + 1, blk):
                s = row[k0 + r2 - j0 : k0 + r2 - j0 + 1, :]
                acc[r2] = acc[r2] - s * row


def local_chol_kernel(nleaf, nb, slots, count, g_ref, p_ref, o_ref, k_ref, T, PT):
    lanes = nb + 1
    for i in range(R):
        T[pl.ds(i * R, R), :] = g_ref[pl.ds(i, lanes, stride=R), :].T
    chol_core(T, lanes)
    for i in range(R):
        o_ref[pl.ds(i, nb, stride=R), :] = T[pl.ds(i * R, R), :].T[:nb]
    half = nleaf // 2

    def put(n, _):
        at = pl.multiple_of(n * R, R)
        k_ref[pl.ds(at, R), :] = jnp.concatenate(
            [o_ref[pl.ds(at, R), :], o_ref[pl.ds(at + half * R, R), :]], axis=1
        )
        return _

    lax.fori_loop(0, half, put, 0, unroll=4)
    for r in range(nleaf):
        PT[3 * r : 3 * r + 3, :] = p_ref[r]
    points = 3 * half
    k_ref[half * R : half * R + points, :] = jnp.concatenate([PT[:points], PT[points:]], axis=1)
    lane = lax.broadcasted_iota(jnp.int32, (8, W), 1)
    chosen = jnp.zeros((8, W), f32)
    live = count[0, 0]
    nslot = slots.shape[1]
    for s in range(nslot):
        leaf = slots[0, jnp.minimum(s, live - 1)]
        chosen = jnp.where(lane == s, leaf.astype(f32), chosen)
    k_ref[half * R + points : half * R + points + 8, :] = chosen


def local_chol(slots, count, grams, points):
    nb = grams.shape[0] - 1
    nleaf = points.shape[0]
    rows = nleaf // 2 * R + 3 * nleaf // 2 + 8
    out, packet = pl.pallas_call(
        functools.partial(local_chol_kernel, nleaf, nb),
        out_shape=(
            jax.ShapeDtypeStruct((nb * R, R), f32),
            jax.ShapeDtypeStruct((rows, W), f32),
        ),
        in_specs=[SM, SM, VM, VM],
        out_specs=(VM, VM),
        scratch_shapes=[pltpu.VMEM((R * R, nb + 1), f32), pltpu.VMEM((3 * nleaf, R), f32)],
        compiler_params=pltpu.CompilerParams(vmem_limit_bytes=FULL),
        cost_estimate=pl.CostEstimate(flops=10**8, bytes_accessed=10**7, transcendentals=0),
        name="local_chol",
    )(slots, count, grams.reshape((nb + 1) * R, R), points)
    return out.reshape(nb, R, R), packet


def group_kernel(axes, levels, base, axes2, levels2, r_ref, own_ref, e_ref, h_ref, s_ref, next_ref, K):
    fs = [e_ref[base + i] for i in range(levels + levels2)]
    grams = receive(levels, lax.axis_index(axes), own_ref[...], r_ref, fs[:levels])
    for i in range(levels):
        h_ref[i] = grams[i]
    next_ref[...] = send(levels2, lax.axis_index(axes2), grams[-1], fs[levels:], K, s_ref)


def group_step(axes, levels, base, axes2, levels2, received, own, path):
    return pl.pallas_call(
        functools.partial(group_kernel, axes, levels, base, axes2, levels2),
        out_shape=(
            jax.ShapeDtypeStruct((levels, R, R), f32),
            jax.ShapeDtypeStruct((2**levels2, R // 2, W), f32),
            jax.ShapeDtypeStruct((R // 2, W), f32),
        ),
        in_specs=[VM, VM, VM],
        out_specs=(VM, VM, VM),
        scratch_shapes=[pltpu.VMEM((levels2, R // 2, W), f32)],
        compiler_params=pltpu.CompilerParams(vmem_limit_bytes=16 * 2**20),
        cost_estimate=pl.CostEstimate(flops=10**7, bytes_accessed=10**6, transcendentals=0),
        name="group_step",
    )(received, own, path)


def path_chol_kernel(axes, levels, base, counts, *refs):
    r_ref, own_ref, e_ref = refs[:3]
    o_ref, T, S = refs[-3:]
    done = 0
    for count, ref in zip(counts, refs[3:-3]):
        for n in range(count):
            S[pl.ds((done + n) * R, R), :] = ref[n]
        done += count
    fs = [e_ref[base + i] for i in range(levels)]
    grams = receive(levels, lax.axis_index(axes), own_ref[...], r_ref, fs)
    total = done + levels
    lanes = S.shape[0] // R
    for n in range(done, lanes):
        S[pl.ds(n * R, R), :] = grams[min(n - done, levels - 1)]
    for i in range(R):
        T[pl.ds(i * R, R), :] = S[pl.ds(i, lanes, stride=R), :].T
    chol_core(T, lanes)
    for i in range(R):
        o_ref[pl.ds(i, total, stride=R), :] = T[pl.ds(i * R, R), :].T[:total]


def path_chol(axes, levels, base, received, own, path, grams):
    counts = [g.shape[0] for g in grams]
    total = sum(counts) + levels
    lanes = (total + 7) // 8 * 8
    out = pl.pallas_call(
        functools.partial(path_chol_kernel, axes, levels, base, counts),
        out_shape=jax.ShapeDtypeStruct((total * R, R), f32),
        in_specs=[VM] * (3 + len(grams)),
        out_specs=VM,
        scratch_shapes=[pltpu.VMEM((R * R, lanes), f32), pltpu.VMEM((lanes * R, R), f32)],
        compiler_params=pltpu.CompilerParams(vmem_limit_bytes=LIMIT),
        cost_estimate=pl.CostEstimate(flops=10**7, bytes_accessed=10**6, transcendentals=0),
        name="path_chol",
    )(received, own, path, *grams)
    return out.reshape(total, R, R)


def pairs_kernel(
    nleaf, npair, rows, cols, offs, k_ref, a_ref, b_ref, o_hbm, RF, CF, PB, Q, S, OT, table, spot, sem, out_sem
):
    half = nleaf // 2
    points = 3 * half
    mark = half * R + points
    for side, r_ref in enumerate((a_ref, b_ref)):
        spot[side] = r_ref[mark : mark + 8, :].astype(jnp.int32)
    copy = pltpu.make_async_copy(spot, table, sem)
    copy.start()

    def prep_row(n, _):
        both = k_ref[pl.ds(pl.multiple_of(n * R, R), R), :]
        RF[n] = both[:, :R]
        RF[half + n] = both[:, R:]
        return _

    lax.fori_loop(0, half, prep_row, 0, unroll=4)
    pt = k_ref[half * R : mark, :].T
    for r in range(points):
        PB[r] = jnp.broadcast_to(pt[:R, r : r + 1], (R, R))
        PB[points + r] = jnp.broadcast_to(pt[R:, r : r + 1], (R, R))
    for side, r_ref in enumerate((a_ref, b_ref)):

        def prep_col(n, _, side=side, r_ref=r_ref):
            both = r_ref[pl.ds(pl.multiple_of(n * R, R), R), :].T
            CF[side * nleaf + n] = both[:R]
            CF[side * nleaf + half + n] = both[R:]
            return _

        lax.fori_loop(0, half, prep_col, 0, unroll=4)
        q = r_ref[half * R : mark, :]
        Q[side * 2 * points : side * 2 * points + points, :] = q[:, :R]
        Q[side * 2 * points + points : (side + 1) * 2 * points, :] = q[:, R:]
    copy.wait()
    odd = lax.axis_index("core")
    wide = 16

    def block(t, _):
        ks = [t * wide + u for u in range(wide)]
        rs = [rows[0, k] for k in ks]
        cs = []
        for k in ks:
            v = cols[0, k]
            right = v // nleaf
            side = jnp.where(odd == 1, right, 1 - right)
            cs.append(side * nleaf + table[side, 0, v % nleaf])
        near = []
        for k, r, c in zip(ks, rs, cs):
            d2 = None
            for a in range(3):
                q = Q[pl.ds(3 * c + a, 1), :] + offs[a, k].astype(f32)
                d = PB[3 * r + a] - q
                d2 = d * d if d2 is None else d2 + d * d
            near.append(lax.rsqrt(d2))
        left = [mm(x, CF[c]) for x, c in zip(near, cs)]
        out = [mm(RF[r], x) for x, r in zip(left, rs)]
        for u in range(wide):
            S[pl.ds(pl.multiple_of(ks[u] * R, R), R), :] = out[u]
        return _

    lax.fori_loop(0, npair // wide, block, 0)
    parts = 4
    rows_each = R // parts
    copies = []
    for c in range(parts):
        for i in range(c * rows_each, (c + 1) * rows_each):
            OT[i] = S[pl.ds(i, npair, stride=R), :].T.astype(bf16)
        at = pl.ds(c * rows_each, rows_each)
        copies.append(pltpu.make_async_copy(OT.at[at], o_hbm.at[at], out_sem.at[c]))
        copies[-1].start()
    for copy in copies:
        copy.wait()


def pairs(rows, cols, offs, packet, first, second, nleaf):
    npair = rows.shape[1]
    out = pl.pallas_call(
        functools.partial(pairs_kernel, nleaf, npair),
        out_shape=jax.ShapeDtypeStruct((R, R, npair), bf16),
        in_specs=[SM, SM, SM, VM, VM, VM],
        out_specs=HB,
        scratch_shapes=[
            pltpu.VMEM((nleaf, R, R), f32),
            pltpu.VMEM((2 * nleaf, R, R), f32),
            pltpu.VMEM((3 * nleaf, R, R), f32),
            pltpu.VMEM((6 * nleaf, R), f32),
            pltpu.VMEM((npair * R, R), f32),
            pltpu.VMEM((R, R, npair), bf16),
            pltpu.SMEM((2, 8, W), jnp.int32),
            pltpu.VMEM((2, 8, W), jnp.int32),
            pltpu.SemaphoreType.DMA,
            pltpu.SemaphoreType.DMA((4,)),
        ],
        compiler_params=pltpu.CompilerParams(vmem_limit_bytes=LIMIT),
        cost_estimate=pl.CostEstimate(flops=10**8, bytes_accessed=10**7, transcendentals=0),
        name="pairs",
    )(rows, cols, offs, packet, first, second)
    return jnp.transpose(out, (2, 0, 1))


LEAF = ("y", "z", "core")


def width(axes):
    return lax.axis_size(axes).bit_length() - 1


def swap(block, axes):
    return lax.all_to_all(block, axes, 0, 0)


def body(
    leaf_bases,
    local_transfer,
    path_transfer,
    leaf_points,
    pair_rows,
    pair_cols,
    pair_offsets,
    send_slots,
    send_counts,
):
    path = path_transfer[0, 0]
    points = leaf_points[0, 0]
    groups = [("core", "sub"), ("z",), ("y",)]
    sizes = [width(axes) for axes in groups]
    grams, mine, own = tree(leaf_bases[0, 0], local_transfer[0, 0], path, groups[0], sizes[0])
    count = lax.axis_size(LEAF)
    inside = [(i, i ^ 1) for i in range(count)]
    across = []
    for i in range(1, count - 1, 2):
        across += [(i, i + 1), (i + 1, i)]

    level_grams = []
    base = 0
    for g in range(len(groups) - 1):
        received = swap(mine, groups[g])
        if g == 1:
            factors, packet = local_chol(send_slots[0], send_counts, grams, points)
            first = lax.ppermute(packet, LEAF, inside)
            second = lax.ppermute(packet, LEAF, across)
            received, packet = lax.optimization_barrier((received, packet))
        done, mine, own = group_step(
            groups[g], sizes[g], base, groups[g + 1], sizes[g + 1], received, own, path
        )
        if g == 0:
            mine, grams = lax.optimization_barrier((mine, grams))
        level_grams.append(done)
        base += sizes[g]
    mine, first, second = lax.optimization_barrier((mine, first, second))
    received = swap(mine, groups[-1])
    couplings = pairs(
        pair_rows[0], pair_cols[0], pair_offsets[0, 0], packet, first, second, points.shape[0]
    )
    received, couplings = lax.optimization_barrier((received, couplings))
    path_factors = path_chol(groups[-1], sizes[-1], base, received, own, path, level_grams)
    return (factors[None, None], path_factors[None, None], couplings[None, None])


def solution(mesh):
    leaves, subs = mesh.devices.shape
    rows = 4 if leaves % 64 == 0 else 2
    parts = Mesh(mesh.devices.reshape(rows, leaves // rows // 2, 2, subs), LEAF + ("sub",))
    wide = P(LEAF, "sub", None, None, None)
    in_specs = (
        wide,
        wide,
        wide,
        wide,
        P(LEAF, "sub", None),
        P(LEAF, "sub", None),
        P(LEAF, "sub", None, None),
        P(LEAF, "sub", None),
        P(LEAF, "sub"),
    )
    return jax.shard_map(body, mesh=parts, in_specs=in_specs, out_specs=(wide, wide, wide), check_vma=False)
```
